32 devices in a mesh: pix: 4 (over y, x), tok: 8 (over z, core).
Axes of the slice: x: 2, y: 2, z: 4, core: 2. Of those that a mesh axis runs over, the one named last changes fastest.
Arguments:
- pixels: bfloat16 [8, 4, 1024, 768], P('tok'), may hold values from -6 to 6
- lengths: int32 [8, 4], P('tok'), may hold values from 256 to 1024, as said below
- base_kernel: bfloat16 [3, 1024, 768], P(None, 'pix'), may hold values from -0.21875 to 0.21875
- resize: bfloat16 [1024, 256], P('pix'), may hold values from -0.1875 to 0.1875
- gain_one: float32 [768], replicated, may hold values from 0.5 to 1.5
- shift_one: float32 [768], replicated, may hold values from -3 to 3
- w_qkv: bfloat16 [768, 2304], replicated, may hold values from -0.21875 to 0.21875
- w_out: bfloat16 [768, 768], replicated, may hold values from -1.75 to 1.75
- gain_two: float32 [768], replicated, may hold values from 0.5 to 1.5
- shift_two: float32 [768], replicated, may hold values from -3 to 3
- w_up: bfloat16 [768, 3072], replicated, may hold values from -0.21875 to 0.21875
- b_up: float32 [3072], replicated, may hold values from -3 to 3
- w_down: bfloat16 [3072, 768], replicated, may hold values from -0.15625 to 0.15625
- cot_act: bfloat16 [8, 4, 1024, 768], P('tok', 'pix'), may hold values from -6 to 6
- cot_pool: float32 [8, 4, 768], P('tok', 'pix'), may hold values from -6 to 6
Outputs:
- activations: bfloat16 [8, 4, 1024, 768], P('tok', 'pix')
- pooled: float32 [8, 4, 768], P('tok', 'pix')
- pixel_grad: float32 [8, 4, 1024, 768], P('tok', 'pix')
- base_grad: float32 [3, 1024, 768], P(None, 'pix')
- grad_gain_one: float32 [768], P(('pix', 'tok'))
- grad_shift_one: float32 [768], P(('pix', 'tok'))
- grad_qkv: float32 [768, 2304], P(('pix', 'tok'))
- grad_out: float32 [768, 768], P(('pix', 'tok'))
- grad_gain_two: float32 [768], P(('pix', 'tok'))
- grad_shift_two: float32 [768], P(('pix', 'tok'))
- grad_up: float32 [768, 3072], P(('pix', 'tok'))
- grad_bias_up: float32 [3072], P(('pix', 'tok'))
- grad_down: float32 [3072, 768], P(('pix', 'tok'))
The draws below stay inside these ranges and needn't reach their ends.
Inputs may be any that keep to these rules, and one draw needn't show every extreme that they name: `lengths`: each image's number of patches; in every group of 4 images one or more have exactly 1024.
All inputs are finite; a program needn't handle non-finite values.
Results may differ from the reference program's by a relative error of at most 0.03.
Values may be sent and summed in bfloat16 or wider, within the bound.
No kernel may reach another device: no remote copies, remote signals or barrier semaphores. Data moves between devices by JAX's collectives and lax.ppermute only.
A program may use at most 320 MiB of HBM per device.

```python
import jax
import jax.numpy as jnp
from jax import lax

D = 768
H = 12
HD = 64
FF = 3072
BASE = 1024
PP = 256
L = 1024
KP = 768
GROUPS = 8
IMG_GROUP = 4


def draw_lengths(key, part):
    key = jax.random.fold_in(key, 11)
    first_key, second_key = jax.random.split(key)
    drawn = jax.random.randint(first_key, (GROUPS, IMG_GROUP), max(1, L // 4), L + 1, dtype=jnp.int32)
    full_slot = jax.random.randint(second_key, (GROUPS,), 0, IMG_GROUP, dtype=jnp.int32)
    positions = jnp.arange(IMG_GROUP, dtype=jnp.int32)[None, :]
    return jnp.where(positions == full_slot[:, None], L, drawn).astype(jnp.int32)


def block_levels(key, dims, pieces, least, top_value):
    def one(position, blocks):
        heights = jax.random.uniform(jax.random.fold_in(jax.random.fold_in(key, 6), position), (blocks,), jnp.float32, least / len(pieces), top_value / len(pieces))
        return jnp.repeat(jnp.exp(heights), dims[position] // blocks).reshape((-1,) + (1,) * (len(dims) - position - 1))

    level = one(*pieces[0])
    for cut in pieces[1:]:
        level = level * one(*cut)
    return level


def scatter_about(stream_key, shape, spread, most, shards=(), kind=jnp.bfloat16):
    factor_of = block_levels(stream_key, shape, shards, -0.22, 0.18) if shards else 1.0
    result = jax.random.normal(stream_key, shape, jnp.float32) * spread * factor_of
    return jnp.minimum(jnp.maximum(result, -most), most).astype(kind)


def setup_inputs(seed: int = 0) -> dict:
    key_list = jax.random.split(jax.random.key(seed), 16)
    pixels = scatter_about(key_list[0], (GROUPS, IMG_GROUP, L, KP), 1.0, 6.0, ((0, 8),))
    lengths = draw_lengths(jax.random.fold_in(key_list[15], 71), 0)
    base_kernel = scatter_about(key_list[2], (3, BASE, D), KP ** -0.5, 0.21875, ((1, 4),))
    resize = scatter_about(key_list[3], (BASE, PP), BASE ** -0.5, 0.1875, ((0, 4),))
    gain_one = jnp.clip(1.0 + 0.1 * jax.random.normal(key_list[4], (D,), jnp.float32), 0.5, 1.5)
    shift_one = scatter_about(key_list[5], (D,), 0.3, 3.0, (), jnp.float32)
    w_qkv = scatter_about(key_list[6], (D, 3 * D), D ** -0.5, 0.21875)
    w_out = scatter_about(key_list[7], (D, D), (D // 64) ** -0.5, 1.75)
    gain_two = jnp.clip(1.0 + 0.1 * jax.random.normal(key_list[8], (D,), jnp.float32), 0.5, 1.5)
    shift_two = scatter_about(key_list[9], (D,), 0.3, 3.0, (), jnp.float32)
    w_up = scatter_about(key_list[10], (D, FF), D ** -0.5, 0.21875)
    b_up = scatter_about(key_list[11], (FF,), 0.5, 3.0, (), jnp.float32)
    w_down = scatter_about(key_list[12], (FF, D), (FF // 2) ** -0.5, 0.15625)
    cot_act = scatter_about(key_list[13], (GROUPS, IMG_GROUP, L, D), 1.0, 6.0, ((0, 8), (1, 4)))
    cot_pool = scatter_about(key_list[14], (GROUPS, IMG_GROUP, D), 1.0, 6.0, ((0, 8), (1, 4)), jnp.float32)
    return {"pixels": pixels, "lengths": lengths, "base_kernel": base_kernel, "resize": resize, "gain_one": gain_one, "shift_one": shift_one, "w_qkv": w_qkv, "w_out": w_out, "gain_two": gain_two, "shift_two": shift_two, "w_up": w_up, "b_up": b_up, "w_down": w_down, "cot_act": cot_act, "cot_pool": cot_pool}


@jax.custom_vjp
def low(v):
    return lax.optimization_barrier(v.astype(jnp.bfloat16)).astype(jnp.float32)

@jax.custom_vjp
def low_back(v):
    return v

def low_keep(v):
    return (low(v), None)

def low_pass(kept, grad):
    return (grad,)

def back_keep(v):
    return (v, None)

def back_low(kept, grad):
    return (low(grad),)
low.defvjp(low_keep, low_pass)
low_back.defvjp(back_keep, back_low)
PRECISE = lax.Precision.HIGHEST
EPSILON = 1e-06

def norm_rows(inputs, gain_vec, shift_vec):
    row_mean = lax.optimization_barrier(jnp.mean(inputs, axis=-1, keepdims=True))
    centered = inputs - row_mean
    variance = lax.optimization_barrier(jnp.mean(centered * centered, axis=-1, keepdims=True))
    return centered * lax.rsqrt(variance + EPSILON) * gain_vec + shift_vec

def attend(packed):
    qkv_rows, usable_row = packed
    queries = qkv_rows[:, :D].reshape(L, H, HD)
    key_rows = qkv_rows[:, D:2 * D].reshape(L, H, HD)
    value_rows = qkv_rows[:, 2 * D:].reshape(L, H, HD)
    scores = low_back(jnp.einsum('qhd,khd->hqk', queries, key_rows, precision=PRECISE) * HD ** (-0.5))
    scores = jnp.where(usable_row[None, None, :], scores, -1e+30)
    peak = lax.optimization_barrier(jnp.max(scores, axis=-1, keepdims=True))
    exponent = jnp.exp(scores - peak)
    attn_probs = low(exponent / lax.optimization_barrier(jnp.sum(exponent, axis=-1, keepdims=True)))
    return jnp.einsum('hqk,khd->qhd', attn_probs, value_rows, precision=PRECISE).reshape(L, D)

def reference(pixels, lengths, base_kernel, resize, gain_one, shift_one, w_qkv, w_out, gain_two, shift_two, w_up, b_up, w_down, cot_act, cot_pool):
    usable = jnp.arange(L, dtype=jnp.int32)[None, None, :] < lengths[:, :, None]
    resize_vals = resize.astype(jnp.float32)

    def forward(pixel_vals, base_vals, gain_a, shift_a, qkv_w, out_w, gain_b, shift_b, up_w, up_bias, down_w):
        kernel = low(jnp.einsum('pq,cpd->cqd', resize_vals, base_vals, precision=PRECISE)).reshape(3 * PP, D)
        embedded = low_back(low(jnp.dot(pixel_vals.reshape(-1, 3 * PP), kernel, precision=PRECISE)))
        normed = low(norm_rows(embedded, gain_a, shift_a))
        qkv_all = low_back(low(jnp.dot(normed, qkv_w, precision=PRECISE)))
        mixed_out = lax.map(jax.checkpoint(attend), (qkv_all.reshape(-1, L, 3 * D), usable.reshape(-1, L)))
        mixed_out = low_back(low(mixed_out.reshape(-1, D)))
        middle = embedded + low_back(jnp.dot(mixed_out, out_w, precision=PRECISE))
        normed_two = low(norm_rows(middle, gain_b, shift_b))
        pre_act = low_back(jnp.dot(normed_two, up_w, precision=PRECISE) + up_bias)
        gelu_out = low_back(low(jax.nn.gelu(pre_act, approximate=False)))
        final_out = middle + low_back(jnp.dot(gelu_out, down_w, precision=PRECISE))
        final_out = final_out.reshape(pixel_vals.shape[:-1] + (D,))
        live_weight = usable.astype(jnp.float32)[..., None]
        patch_count = lax.optimization_barrier(jnp.sum(live_weight, axis=2))
        masked = final_out * live_weight
        return (masked, lax.optimization_barrier(jnp.sum(masked, axis=2)) / patch_count)
    primals = (pixels.astype(jnp.float32), base_kernel.astype(jnp.float32), gain_one, shift_one, w_qkv.astype(jnp.float32), w_out.astype(jnp.float32), gain_two, shift_two, w_up.astype(jnp.float32), b_up, w_down.astype(jnp.float32))
    results, pull_back = jax.vjp(forward, *primals)
    gradients = pull_back((cot_act.astype(jnp.float32), cot_pool))
    return (results[0].astype(jnp.bfloat16), results[1], gradients[0], gradients[1], gradients[2], gradients[3], gradients[4], gradients[5], gradients[6], gradients[7], gradients[8], gradients[9], gradients[10])
```

```python
import functools

import jax
import jax.numpy as jnp
from jax import lax
from jax.experimental import pallas as pl
from jax.experimental.pallas import tpu as pltpu
from jax.sharding import PartitionSpec as P

HD = 64
EPSILON = 1e-06
LOG2E = 1.4426950408889634
LN2 = 0.6931471805599453
ROWS = 256
MIB = 1 << 20
BF = jnp.bfloat16
F32 = jnp.float32


def mm(lhs, rhs, lhs_dim, rhs_dim):
    return lax.dot_general(
        lhs, rhs, (((lhs_dim,), (rhs_dim,)), ((), ())), preferred_element_type=F32
    )


def call(body, grid, prefetch, in_specs, out_specs, out_shape, args, flops, scratch=(), vmem=48):
    moved = sum(a.size * a.dtype.itemsize for a in args)
    moved += sum(o.size * o.dtype.itemsize for o in jax.tree.leaves(out_shape))
    return pl.pallas_call(
        body,
        grid_spec=pltpu.PrefetchScalarGridSpec(
            num_scalar_prefetch=len(prefetch),
            grid=grid,
            in_specs=in_specs,
            out_specs=out_specs,
            scratch_shapes=list(scratch),
        ),
        out_shape=out_shape,
        compiler_params=pltpu.CompilerParams(
            dimension_semantics=("arbitrary",) * len(grid), vmem_limit_bytes=vmem * MIB
        ),
        cost_estimate=pl.CostEstimate(
            flops=int(flops), bytes_accessed=int(moved), transcendentals=0
        ),
    )(*prefetch, *args)


def shape(dims, dtype):
    return jax.ShapeDtypeStruct(dims, dtype)


def fixed(dims):
    zeros = (0,) * len(dims)
    return pl.BlockSpec(dims, lambda *a: zeros, pipeline_mode=pl.Buffered(1))


def row_stats(x):
    mean = jnp.mean(x, axis=-1, keepdims=True)
    centered = x - mean
    var = jnp.mean(centered * centered, axis=-1, keepdims=True)
    scale = lax.rsqrt(var + EPSILON)
    return centered * scale, scale


def norm_back(grad, normal, scale, gain):
    e = grad * gain
    mean_e = jnp.mean(e, axis=-1, keepdims=True)
    mean_en = jnp.mean(e * normal, axis=-1, keepdims=True)
    return scale * (e - mean_e - normal * mean_en)


def usable_rows(rows, length):
    start = pl.program_id(0) * rows
    index = lax.broadcasted_iota(jnp.int32, (rows, 1), 0) + start
    return (index < length).astype(F32)


def partial_body(info, resize, base, out):
    out[...] = mm(resize[...], base[0], 0, 0).astype(BF)


def partial_kernel(info, resize, base):
    channels, pixels, width = base.shape
    patch = resize.shape[1]
    half = width // 2
    return call(
        partial_body,
        (channels,),
        (info,),
        [
            fixed((pixels, patch)),
            pl.BlockSpec((1, pixels, half), lambda c, s: (c, 0, s[1])),
        ],
        pl.BlockSpec((patch, half), lambda c, s: (c, 0)),
        shape((channels * patch, half), BF),
        (resize, base),
        2 * channels * pixels * patch * half,
    )


def cot_body(info, cot_act, cot_pool, w_down, branch, grad_gelu):
    length = info[2]
    live = usable_rows(branch.shape[0], length)
    pooled = cot_pool[...] / length.astype(F32)
    value = ((cot_act[0, 0].astype(F32) + pooled) * live).astype(BF)
    branch[...] = value
    grad_gelu[...] = mm(value, w_down[...], 1, 1).astype(BF)


def cot_branch(info, cot_act, cot_pool, w_down):
    rows, width = cot_act.shape[2:]
    hidden = w_down.shape[0]
    return call(
        cot_body,
        (rows // ROWS,),
        (info,),
        [
            pl.BlockSpec((1, 1, ROWS, width), lambda i, s: (0, 0, i, 0)),
            fixed((1, width)),
            fixed((hidden, width)),
        ],
        [
            pl.BlockSpec((ROWS, width), lambda i, s: (i, 0)),
            pl.BlockSpec((ROWS, hidden), lambda i, s: (i, 0)),
        ],
        [shape((rows, width), BF), shape((rows, hidden), BF)],
        (cot_act, cot_pool, w_down),
        2 * rows * width * hidden,
    )


def embed_body(info, pixels, kernel, gain, shift, w_qkv, embedded, normed, qkv):
    width = embedded.shape[1]
    value = mm(pixels[0, 0], kernel[...], 1, 0).astype(BF)
    embedded[...] = value
    normal, _ = row_stats(value.astype(F32))
    low = (normal * gain[...] + shift[...]).astype(BF)
    normed[...] = low
    for part in range(3):
        cols = slice(part * width, (part + 1) * width)
        product = mm(low, w_qkv[:, cols], 1, 0)
        if part == 0:
            product = product * (HD**-0.5 * LOG2E)
        qkv[:, cols] = product.astype(BF)


def embed_rows(info, pixels, kernel, gain, shift, w_qkv):
    rows, patch = pixels.shape[2:]
    width, triple = w_qkv.shape
    return call(
        embed_body,
        (rows // ROWS,),
        (info,),
        [
            pl.BlockSpec((1, 1, ROWS, patch), lambda i, s: (0, s[0], i, 0)),
            fixed((patch, width)),
            fixed((1, width)),
            fixed((1, width)),
            fixed((width, triple)),
        ],
        [
            pl.BlockSpec((ROWS, width), lambda i, s: (i, 0)),
            pl.BlockSpec((ROWS, width), lambda i, s: (i, 0)),
            pl.BlockSpec((ROWS, triple), lambda i, s: (i, 0)),
        ],
        [shape((rows, width), BF), shape((rows, width), BF), shape((rows, triple), BF)],
        (pixels, kernel, gain, shift, w_qkv),
        2 * rows * width * (patch + triple),
    )


def attend_body(q, k, v, extra, probs, mixed, inverse, mixed_t):
    rows = q.shape[0]
    lane = lax.broadcasted_iota(jnp.int32, (1, 2 * HD), 1)
    q_t = q[...].T
    v_t = v[...].T
    first_row = lax.broadcasted_iota(jnp.int32, (HD, rows), 0) == 0
    ones = jnp.where(first_row, 1.0, 0.0).astype(BF)
    for head in range(2):
        own = slice(head * HD, (head + 1) * HD)
        chosen = jnp.where((lane >= HD) == (head == 1), 1.0, 0.0).astype(BF)
        k_own = k[...] * chosen + extra[head]
        stack = [q_t[own], ones] if head == 0 else [ones, q_t[own]]
        q_own = jnp.concatenate(stack, axis=0)
        for start in range(0, rows, ROWS):
            cols = slice(start, start + ROWS)
            scores = mm(k_own, q_own[:, cols], 1, 0)
            peak = jnp.max(scores, axis=0, keepdims=True)
            power = jnp.exp2(scores - peak)
            total = 1.0 / jnp.sum(power, axis=0, keepdims=True)
            low = power.astype(BF)
            probs[head, :, cols] = low
            inverse[0, head : head + 1, cols] = total
            mixed_t[own, cols] = mm(v_t[own], low, 1, 0) * total
    mixed[...] = mixed_t[...].T.astype(BF)


def attend(qkv, extra):
    rows, triple = qkv.shape
    width = triple // 3
    pairs = width // (2 * HD)
    return call(
        attend_body,
        (pairs,),
        (),
        [
            pl.BlockSpec((rows, 2 * HD), lambda j: (0, j)),
            pl.BlockSpec((rows, 2 * HD), lambda j: (0, pairs + j)),
            pl.BlockSpec((rows, 2 * HD), lambda j: (0, 2 * pairs + j)),
            fixed((2, rows, 2 * HD)),
        ],
        [
            pl.BlockSpec((2, rows, rows), lambda j: (j, 0, 0)),
            pl.BlockSpec((rows, 2 * HD), lambda j: (0, j)),
            pl.BlockSpec((1, 2, rows), lambda j: (j, 0, 0)),
        ],
        [
            shape((2 * pairs, rows, rows), BF),
            shape((rows, width), BF),
            shape((pairs, 2, rows), F32),
        ],
        (qkv, qkv, qkv, extra),
        2 * 2 * rows * rows * 256 * 2 * pairs,
        scratch=[pltpu.VMEM((2 * HD, rows), F32)],
    )


def attend_back_body(probs, q, k, v, grad, mixed, inverse, dq, dk, dv, dq_t, score_grad):
    rows = q.shape[0]
    lane = lax.broadcasted_iota(jnp.int32, (1, 2 * HD), 1)
    index = lax.broadcasted_iota(jnp.int32, (HD, rows), 0)
    grad_t = grad[...].T.astype(F32)
    mixed_t = mixed[...].T.astype(F32)
    k_t = k[...].T
    scaled = []
    sides = []
    for head in range(2):
        own = slice(head * HD, (head + 1) * HD)
        total = inverse[0, head : head + 1, :]
        scaled.append((grad_t[own] * total).astype(BF))
        inner = -jnp.sum(grad_t[own] * mixed_t[own], axis=0, keepdims=True) * total
        high = inner.astype(BF).astype(F32)
        sides.append(
            jnp.where(index == 0, high, jnp.where(index == 1, inner - high, 0.0)).astype(BF)
        )
    grad_low = jnp.concatenate(scaled, axis=0).T
    dk_sum = None
    dv_sum = None
    for head in range(2):
        own = slice(head * HD, (head + 1) * HD)
        other = (1 - head) * HD
        chosen = jnp.where((lane >= HD) == (head == 1), 1.0, 0.0).astype(BF)
        units = jnp.where((lane == other) | (lane == other + 1), 1.0, 0.0).astype(BF)
        v_own = v[...] * chosen + units
        stack = [scaled[0], sides[0]] if head == 0 else [sides[1], scaled[1]]
        right = jnp.concatenate(stack, axis=0)
        for start in range(0, rows, ROWS):
            cols = slice(start, start + ROWS)
            shifted = mm(v_own, right[:, cols], 1, 0)
            low = (probs[head, :, cols].astype(F32) * shifted).astype(BF)
            score_grad[:, cols] = low
            dq_t[own, cols] = mm(k_t[own], low, 1, 0)
        dv_part = mm(probs[head], grad_low * chosen, 1, 0)
        dk_part = mm(score_grad[...], q[...] * chosen, 1, 0)
        dv_sum = dv_part if dv_sum is None else dv_sum + dv_part
        dk_sum = dk_part if dk_sum is None else dk_sum + dk_part
    dq[...] = (dq_t[...] * (HD**-0.5)).T.astype(BF)
    dk[...] = (dk_sum * LN2).astype(BF)
    dv[...] = dv_sum.astype(BF)


def attend_back(probs, qkv, grad_mixed, mixed, inverse):
    rows, triple = qkv.shape
    width = triple // 3
    pairs = width // (2 * HD)
    column = pl.BlockSpec((rows, 2 * HD), lambda j: (0, j))
    return call(
        attend_back_body,
        (pairs,),
        (),
        [
            pl.BlockSpec((2, rows, rows), lambda j: (j, 0, 0)),
            column,
            pl.BlockSpec((rows, 2 * HD), lambda j: (0, pairs + j)),
            pl.BlockSpec((rows, 2 * HD), lambda j: (0, 2 * pairs + j)),
            column,
            column,
            pl.BlockSpec((1, 2, rows), lambda j: (j, 0, 0)),
        ],
        [column, column, column],
        [shape((rows, width), BF)] * 3,
        (probs, qkv, qkv, qkv, grad_mixed, mixed, inverse),
        4 * 2 * rows * rows * 256 * 2 * pairs,
        scratch=[pltpu.VMEM((2 * HD, rows), F32), pltpu.VMEM((rows, rows), BF)],
    )


def gelu_parts(x):
    size = jnp.abs(x)
    t = 1.0 / (1.0 + (0.3275911 * 0.7071067811865476) * size)
    bell = jnp.exp2((-0.5 * LOG2E) * x * x)
    series = t * (
        0.127414796
        + t * (-0.142248368 + t * (0.7107068705 + t * (-0.7265760135 + t * 0.5307027145)))
    )
    tail = series * bell
    below = jnp.where(x > 0, 1.0 - tail, tail)
    return x * below, below + x * (bell * 0.3989422804014327)


def middle_body(
    info,
    mixed,
    embedded,
    grad_gelu,
    cot_act,
    cot_pool,
    w_out,
    gain,
    shift,
    w_up,
    b_up,
    middle,
    normed,
    gelu_out,
    grad_pre,
    grad_middle,
    grad_attn,
    grad_mixed,
    sums,
    bias_sum,
):
    rows, width = middle.shape
    hidden = w_up.shape[1]
    step = width

    @pl.when(pl.program_id(0) == 0)
    def _():
        sums[...] = jnp.zeros_like(sums)
        bias_sum[...] = jnp.zeros_like(bias_sum)

    value = embedded[...].astype(F32) + mm(mixed[...], w_out[...], 1, 0)
    middle[...] = value
    normal, scale = row_stats(value)
    low = (normal * gain[...] + shift[...]).astype(BF)
    normed[...] = low
    grad_normed = None
    for start in range(0, hidden, step):
        cols = slice(start, start + step)
        pre = mm(low, w_up[:, cols], 1, 0) + b_up[:, cols]
        out, slope = gelu_parts(pre)
        gelu_out[:, cols] = out.astype(BF)
        back = (grad_gelu[:, cols].astype(F32) * slope).astype(BF)
        grad_pre[:, cols] = back
        bias_sum[:, cols] += jnp.sum(back.astype(F32), axis=0, keepdims=True)
        part = mm(back, w_up[:, cols], 1, 1)
        grad_normed = part if grad_normed is None else grad_normed + part
    sums[0:1, :] += jnp.sum(grad_normed * normal, axis=0, keepdims=True)
    sums[1:2, :] += jnp.sum(grad_normed, axis=0, keepdims=True)
    length = info[2]
    live = usable_rows(rows, length)
    pooled = cot_pool[...] / length.astype(F32)
    final = (cot_act[0, 0].astype(F32) + pooled) * live
    total = final + norm_back(grad_normed, normal, scale, gain[...])
    grad_middle[...] = total
    total_low = total.astype(BF)
    grad_attn[...] = total_low
    grad_mixed[...] = mm(total_low, w_out[...], 1, 1).astype(BF)


def middle_rows(
    info, mixed, embedded, grad_gelu, cot_act, cot_pool, w_out, gain, shift, w_up, b_up
):
    rows, width = mixed.shape
    hidden = w_up.shape[1]
    narrow = pl.BlockSpec((ROWS, width), lambda i, s: (i, 0))
    wide = pl.BlockSpec((ROWS, hidden), lambda i, s: (i, 0))
    return call(
        middle_body,
        (rows // ROWS,),
        (info,),
        [
            narrow,
            narrow,
            wide,
            pl.BlockSpec((1, 1, ROWS, width), lambda i, s: (0, 0, i, 0)),
            fixed((1, width)),
            fixed((width, width)),
            fixed((1, width)),
            fixed((1, width)),
            fixed((width, hidden)),
            fixed((1, hidden)),
        ],
        [narrow, narrow, wide, wide, narrow, narrow, narrow]
        + [
            pl.BlockSpec((8, width), lambda i, s: (0, 0)),
            pl.BlockSpec((1, hidden), lambda i, s: (0, 0)),
        ],
        [
            shape((rows, width), F32),
            shape((rows, width), BF),
            shape((rows, hidden), BF),
            shape((rows, hidden), BF),
            shape((rows, width), F32),
            shape((rows, width), BF),
            shape((rows, width), BF),
            shape((8, width), F32),
            shape((1, hidden), F32),
        ],
        (mixed, embedded, grad_gelu, cot_act, cot_pool, w_out, gain, shift, w_up, b_up),
        2 * rows * width * (2 * width + 2 * hidden),
    )


def fold_columns(block, shards, folds):
    height = block.shape[0] // (shards * folds)
    rows = []
    for i in range(shards):
        parts = [
            block[(i * folds + j) * height : (i * folds + j + 1) * height] for j in range(folds)
        ]
        rows.append(jnp.concatenate(parts, axis=1))
    return jnp.concatenate(rows, axis=0)


def down_body(order, which, left, right, *refs):
    out = mm(left[...], right[...], 0, 0)
    if len(refs) == 1:
        refs[0][0] = out.astype(BF)
        return
    arrived, away, keep = refs
    out = (out + arrived[0].astype(F32)).astype(BF)
    step = pl.program_id(0)

    @pl.when(step < 2)
    def _():
        away[0] = out

    @pl.when(step >= 2)
    def _():
        keep[0] = out


def grad_down_half(order, which, gelu_out, branch, arrived=None):
    rows, hidden = gelu_out.shape
    half = branch.shape[1] // 2
    tall = hidden // 4
    specs = [
        pl.BlockSpec((rows, tall), lambda j, o, w: (0, o[j])),
        pl.BlockSpec((rows, half), lambda j, o, w: (0, w[0])),
    ]
    args = (gelu_out, branch)
    block = (1, tall, half)
    flops = 2 * rows * hidden * half
    if arrived is None:
        return call(
            down_body,
            (4,),
            (order, which),
            specs,
            pl.BlockSpec(block, lambda j, o, w: (j, 0, 0)),
            shape((4, tall, half), BF),
            args,
            flops,
        )
    return call(
        down_body,
        (4,),
        (order, which),
        specs + [pl.BlockSpec(block, lambda j, o, w: (j, 0, 0))],
        [
            pl.BlockSpec(block, lambda j, o, w: (jnp.minimum(j, 1), 0, 0)),
            pl.BlockSpec(block, lambda j, o, w: (jnp.maximum(j - 2, 0), 0, 0)),
        ],
        [shape((2, tall, half), BF)] * 2,
        args + (arrived,),
        flops,
    )


def place_quarters(order, work, refs, lanes):
    for j in range(4):
        block = work[order[j], :, lanes]
        if len(refs) == 1:
            refs[0][j, :, lanes] = block.astype(BF)
        else:
            arrived, away, keep = refs
            block = (block + arrived[j, :, lanes].astype(F32)).astype(BF)
            if j < 2:
                away[j, :, lanes] = block
            else:
                keep[j - 2, :, lanes] = block


def spread(work, lanes, value):
    quarter = work.shape[1]
    for i in range(4):
        work[i, :, lanes] = value[i * quarter : (i + 1) * quarter]


def turned(vectors):
    pad = jnp.zeros((120, vectors.shape[1]), F32)
    return jnp.concatenate([vectors, pad], axis=0).T


def up_body(order, which, normed, grad_pre, mixed, grad_attn, vectors, *refs):
    refs, work = refs[:-1], refs[-1]
    step = pl.program_id(0)
    last = pl.num_programs(0) - 1
    lanes = work.shape[2]
    half = grad_attn.shape[1]

    @pl.when(step < last)
    def _():
        spread(work, slice(0, lanes), mm(normed[...], grad_pre[...], 0, 0))

    @pl.when(step == last)
    def _():
        spread(work, slice(0, half), mm(mixed[...], grad_attn[...], 0, 0))
        spread(work, slice(half, lanes), turned(vectors[...]))

    place_quarters(order, work, refs, slice(0, lanes))


def column_call(body, order, which, grid, lanes, quarter, specs, args, flops, arrived):
    total = grid * lanes
    if arrived is None:
        out_specs = pl.BlockSpec((4, quarter, lanes), lambda j, o, w: (0, 0, j))
        out_shape = shape((4, quarter, total), BF)
    else:
        specs = specs + [pl.BlockSpec((4, quarter, lanes), lambda j, o, w: (0, 0, j))]
        args = args + (arrived,)
        out_specs = [pl.BlockSpec((2, quarter, lanes), lambda j, o, w: (0, 0, j))] * 2
        out_shape = [shape((2, quarter, total), BF)] * 2
    return call(
        body,
        (grid,),
        (order, which),
        specs,
        out_specs,
        out_shape,
        args,
        flops,
        scratch=[pltpu.VMEM((4, quarter, lanes), F32)],
    )


def grad_up_half(order, which, normed, grad_pre, mixed, grad_attn, vectors, arrived=None):
    rows, width = normed.shape
    half = width // 2
    lanes = half + 128
    steps = grad_pre.shape[1] // 2 // lanes
    specs = [
        fixed((rows, width)),
        pl.BlockSpec(
            (rows, lanes), lambda j, o, w: (0, w[0] * steps + jnp.minimum(j, steps - 1))
        ),
        fixed((rows, width)),
        pl.BlockSpec((rows, half), lambda j, o, w: (0, w[0])),
        fixed(vectors.shape),
    ]
    return column_call(
        up_body,
        order,
        which,
        steps + 1,
        lanes,
        width // 4,
        specs,
        (normed, grad_pre, mixed, grad_attn, vectors),
        2 * rows * width * (steps * lanes + half),
        arrived,
    )


def qkv_body(order, which, normed, dq, dk, dv, *refs):
    refs, work = refs[:-1], refs[-1]
    step = pl.program_id(0)
    for i, part in enumerate((dq, dk, dv)):

        @pl.when(step == i)
        def _(part=part):
            spread(work, slice(None), mm(normed[...], part[...], 0, 0))

    place_quarters(order, work, refs, slice(None))


def grad_qkv_half(order, which, normed, parts, arrived=None):
    rows, width = normed.shape
    half = width // 2
    specs = [fixed((rows, width))]
    specs += [pl.BlockSpec((rows, half), lambda j, o, w: (0, w[0]))] * 3
    return column_call(
        qkv_body,
        order,
        which,
        3,
        half,
        width // 4,
        specs,
        (normed,) + tuple(parts),
        2 * rows * width * 3 * half,
        arrived,
    )


def kernel_body(order, which, pixels, grad, vectors, *refs):
    refs, work = refs[:-1], refs[-1]
    half = grad.shape[1]
    spread(work, slice(0, half), mm(pixels[0, 0], grad[...], 0, 0))
    spread(work, slice(half, half + 128), turned(vectors[...]))
    place_quarters(order, work, refs, slice(None))


def grad_kernel_half(order, which, pixels, grad, vectors, arrived=None):
    rows, patch = pixels.shape[2:]
    half = grad.shape[1] // 2
    specs = [
        pl.BlockSpec((1, 1, rows, patch), lambda j, o, w: (0, w[1], 0, 0)),
        pl.BlockSpec((rows, half), lambda j, o, w: (0, w[0])),
        fixed(vectors.shape),
    ]
    return column_call(
        kernel_body,
        order,
        which,
        1,
        half + 128,
        patch // 4,
        specs,
        (pixels, grad, vectors),
        2 * rows * patch * half,
        arrived,
    )


def first_back_body(dq, dk, dv, w_qkv, embedded, gain, grad_middle, out, sums):
    width = out.shape[1]

    @pl.when(pl.program_id(0) == 0)
    def _():
        sums[...] = jnp.zeros_like(sums)

    grad = mm(dq[...], w_qkv[:, :width], 1, 1)
    grad += mm(dk[...], w_qkv[:, width : 2 * width], 1, 1)
    grad += mm(dv[...], w_qkv[:, 2 * width :], 1, 1)
    normal, scale = row_stats(embedded[...].astype(F32))
    sums[0:1, :] += jnp.sum(grad * normal, axis=0, keepdims=True)
    sums[1:2, :] += jnp.sum(grad, axis=0, keepdims=True)
    out[...] = (grad_middle[...] + norm_back(grad, normal, scale, gain[...])).astype(BF)


def first_back(parts, w_qkv, embedded, gain, grad_middle):
    rows, width = embedded.shape
    narrow = pl.BlockSpec((ROWS, width), lambda i: (i, 0))
    return call(
        first_back_body,
        (rows // ROWS,),
        (),
        [narrow] * 3 + [fixed(w_qkv.shape), narrow, fixed((1, width)), narrow],
        [narrow, pl.BlockSpec((8, width), lambda i: (0, 0))],
        [shape((rows, width), BF), shape((8, width), F32)],
        tuple(parts) + (w_qkv, embedded, gain, grad_middle),
        2 * rows * width * 3 * width,
    )


def last_body(
    info, middle, gelu_out, w_down, grad_embedded, kernel, activations, pooled, pixel_grad
):
    rows = middle.shape[0]
    length = info[2]

    @pl.when(pl.program_id(0) == 0)
    def _():
        pooled[...] = jnp.zeros_like(pooled)

    pixel_grad[0, 0] = mm(grad_embedded[...], kernel[...], 1, 1)
    final = middle[...] + mm(gelu_out[...], w_down[...], 1, 0)
    final = final * usable_rows(rows, length)
    activations[0, 0] = final.astype(BF)
    pooled[0] += jnp.sum(final, axis=0, keepdims=True)

    @pl.when(pl.program_id(0) == pl.num_programs(0) - 1)
    def _():
        pooled[...] = pooled[...] / length.astype(F32)


def last_rows(info, middle, gelu_out, w_down, grad_embedded, kernel):
    rows, width = middle.shape
    hidden = w_down.shape[0]
    patch = kernel.shape[0]
    narrow = pl.BlockSpec((ROWS, width), lambda i, s: (i, 0))
    return call(
        last_body,
        (rows // ROWS,),
        (info,),
        [
            narrow,
            pl.BlockSpec((ROWS, hidden), lambda i, s: (i, 0)),
            fixed((hidden, width)),
            narrow,
            fixed((patch, width)),
        ],
        [
            pl.BlockSpec((1, 1, ROWS, width), lambda i, s: (0, 0, i, 0)),
            pl.BlockSpec((1, 1, width), lambda i, s: (0, 0, 0)),
            pl.BlockSpec((1, 1, ROWS, patch), lambda i, s: (0, 0, i, 0)),
        ],
        [
            shape((1, 1, rows, width), BF),
            shape((1, 1, width), F32),
            shape((1, 1, rows, patch), F32),
        ],
        (middle, gelu_out, w_down, grad_embedded, kernel),
        2 * rows * width * (hidden + patch),
    )


def base_body(order, order_far, which, resize, near, far, out, work):
    half = near.shape[2]
    quarter = near.shape[1]
    patch = resize.shape[1]
    for j in range(4):
        rows = pl.ds(pl.multiple_of(order[j] * quarter, quarter), quarter)
        work[which[0], rows, :] = near[j]
        rows = pl.ds(pl.multiple_of(order_far[j] * quarter, quarter), quarter)
        work[1 - which[0], rows, :] = far[j]
    for c in range(out.shape[0]):
        for h in range(2):
            out[c, :, h * half : (h + 1) * half] = mm(
                resize[...], work[h, c * patch : (c + 1) * patch, :], 1, 0
            )


def base_grad_of(order, order_far, which, resize, near, far, channels):
    pixels, patch = resize.shape
    _, quarter, half = near.shape
    return call(
        base_body,
        (1,),
        (order, order_far, which),
        [fixed(resize.shape), fixed(near.shape), fixed(far.shape)],
        fixed((channels, pixels, 2 * half)),
        shape((channels, pixels, 2 * half), F32),
        (resize, near, far),
        2 * channels * pixels * patch * 2 * half,
        scratch=[pltpu.VMEM((2, 4 * quarter, half), BF)],
    )


class Links:
    def __init__(self):
        self.parts = lax.axis_size("pix")
        self.count = lax.axis_size("tok")
        self.pix = lax.axis_index("pix")
        self.tok = lax.axis_index("tok")
        self.core = self.tok % 2
        self.chips = self.count // 2
        self.near = 1 + self.core
        self.far = 2 - self.core

    def swap(self, value, partner):
        pairs = []
        for p in range(self.parts):
            for t in range(self.count):
                q, u = partner(p, t)
                pairs.append((p * self.count + t, q * self.count + u))
        return lax.ppermute(value, ("pix", "tok"), pairs)

    def core_swap(self, value):
        return self.swap(value, lambda p, t: (p, t ^ 1))

    def first_swap(self, value):
        return self.swap(value, lambda p, t: (p ^ (1 + t % 2), t))

    def second_swap(self, value):
        return self.swap(value, lambda p, t: (p ^ (2 - t % 2), t))

    def chip_swap(self, value, bit):
        return self.swap(value, lambda p, t: (p, t ^ (2 << bit)))

    def quarters(self, near, far):
        pix = self.pix
        return jnp.stack([pix ^ near, pix ^ 3, pix, pix ^ far]).astype(jnp.int32)


def add(a, b, dtype=BF):
    return (a.astype(F32) + b.astype(F32)).astype(dtype)


def reduce_quarter(links, away, keep):
    arrived = links.first_swap(away)
    leaving = add(arrived[1], keep[1])
    staying = add(arrived[0], keep[0])
    return add(links.second_swap(leaving), staying)


def reduce_chips(links, block, height):
    value = block.reshape(links.chips, height, block.shape[-1])
    bits = links.chips.bit_length() - 1
    for bit in range(bits):
        own = (links.tok >> (bit + 1)) & 1
        value = value.reshape(value.shape[0] // 2, 2, height, value.shape[-1])
        leaving = lax.dynamic_index_in_dim(value, 1 - own, 1, keepdims=False)
        staying = lax.dynamic_index_in_dim(value, own, 1, keepdims=False)
        value = add(links.chip_swap(leaving, bit), staying, F32 if bit == bits - 1 else BF)
    return value.reshape(height, value.shape[-1])


def own_rows(links, block):
    pair = block.reshape(2, block.shape[0] // 2, block.shape[1])
    mine = lax.dynamic_index_in_dim(pair, links.core, 0, keepdims=False)
    arrived = links.core_swap(
        lax.dynamic_index_in_dim(pair, 1 - links.core, 0, keepdims=False)
    )
    first = links.core == 0
    return jnp.where(first, mine, arrived), jnp.where(first, arrived, mine)


def local(
    pixels,
    lengths,
    base_kernel,
    resize,
    gain_one,
    shift_one,
    w_qkv,
    w_out,
    gain_two,
    shift_two,
    w_up,
    b_up,
    w_down,
    cot_act,
    cot_pool,
):
    links = Links()
    seq_len = pixels.shape[2]
    width = w_qkv.shape[0]
    hidden = w_up.shape[1]
    channels = base_kernel.shape[0]
    half = width // 2
    core = links.core
    own_length = lax.dynamic_index_in_dim(lengths[0], links.pix, 0, keepdims=False)
    info = jnp.stack([links.pix, core, own_length]).astype(jnp.int32)
    mine = jnp.stack([core, links.pix]).astype(jnp.int32)
    theirs = jnp.stack([1 - core, links.pix]).astype(jnp.int32)
    order = links.quarters(links.near, links.far)
    order_theirs = links.quarters(links.far, links.near)
    gain_one, shift_one = gain_one[None], shift_one[None]
    gain_two, shift_two, b_up = gain_two[None], shift_two[None], b_up[None]
    cot_pool = cot_pool[0]

    piece = partial_kernel(info, resize, base_kernel)
    piece = add(links.first_swap(piece), piece)
    piece = add(links.second_swap(piece), piece)
    other = links.core_swap(piece)
    kernel = jnp.concatenate(
        [jnp.where(core == 0, piece, other), jnp.where(core == 0, other, piece)], axis=1
    )
    branch, grad_gelu = cot_branch(info, cot_act, cot_pool, w_down)

    lane = jnp.arange(2 * HD)[None, None, :]
    slot = jnp.array([HD, 0])[:, None, None]
    blocked = (jnp.arange(seq_len) >= own_length)[None, :, None] & (lane == slot)
    extra = jnp.where(blocked, -1e30, 0.0).astype(BF)

    embedded, normed, qkv = embed_rows(info, pixels, kernel, gain_one, shift_one, w_qkv)
    probs, mixed, inverse = attend(qkv, extra)
    (
        middle,
        normed_two,
        gelu_out,
        grad_pre,
        grad_middle,
        grad_attn,
        grad_mixed,
        sums_two,
        bias_sum,
    ) = middle_rows(
        info, mixed, embedded, grad_gelu, cot_act, cot_pool, w_out, gain_two, shift_two, w_up, b_up
    )

    fold = hidden // width
    vectors_two = jnp.concatenate(
        [sums_two[:2], bias_sum.reshape(width, fold).T, jnp.zeros((6 - fold, width), F32)], axis=0
    )
    down_away = grad_down_half(order_theirs, theirs, gelu_out, branch)
    down_arrived = links.core_swap(down_away)
    up_args = (normed_two, grad_pre, mixed, grad_attn, vectors_two)
    up_arrived = links.core_swap(grad_up_half(order_theirs, theirs, *up_args))
    down_away, down_keep = grad_down_half(order, mine, gelu_out, branch, down_arrived)
    up_away, up_keep = grad_up_half(order, mine, *up_args, up_arrived)
    down = reduce_quarter(links, down_away, down_keep)
    up = reduce_quarter(links, up_away, up_keep)
    down = reduce_chips(links, down, hidden // (links.parts * links.chips))
    up = reduce_chips(links, up, width // (links.parts * links.chips))

    parts = attend_back(probs, qkv, grad_mixed, mixed, inverse)

    qkv_arrived = links.core_swap(grad_qkv_half(order_theirs, theirs, normed, parts))
    qkv_away, qkv_keep = grad_qkv_half(order, mine, normed, parts, qkv_arrived)
    three = reduce_quarter(links, qkv_away, qkv_keep)
    three = reduce_chips(links, three, width // (links.parts * links.chips))

    grad_embedded, vectors_one = first_back(parts, w_qkv, embedded, gain_one, grad_middle)
    kernel_args = (pixels, grad_embedded, vectors_one)
    kernel_arrived = links.core_swap(grad_kernel_half(order_theirs, theirs, *kernel_args))
    kernel_away, kernel_keep = grad_kernel_half(order, mine, *kernel_args, kernel_arrived)
    quarter = reduce_quarter(links, kernel_away, kernel_keep)
    for bit in range(links.chips.bit_length() - 1):
        quarter = add(links.chip_swap(quarter, bit), quarter)
    vector_cols = quarter[:, half:]
    quarter = quarter[:, :half]
    pair = jnp.stack([quarter, links.second_swap(quarter)])
    full = jnp.concatenate([links.first_swap(pair), pair], axis=0)
    base_grad = base_grad_of(
        order, order_theirs, mine, resize, full, links.core_swap(full), channels
    )

    activations, pooled, pixel_grad = last_rows(
        info, middle, gelu_out, w_down, grad_embedded, kernel
    )

    height = width // (links.parts * links.count)
    tall = hidden // (links.parts * links.count)
    down = jnp.concatenate(own_rows(links, down), axis=1)
    up_cols = hidden // 2
    up_low, up_high = own_rows(links, up)
    grad_up = jnp.concatenate([up_low[:, :up_cols], up_high[:, :up_cols]], axis=1)
    out_cols = slice(up_cols, up_cols + half)
    grad_out = jnp.concatenate([up_low[:, out_cols], up_high[:, out_cols]], axis=1)
    small_two = up_low[:, up_cols + half :]
    three_low, three_high = own_rows(links, three)
    grad_qkv = jnp.concatenate(
        [
            x[:, i * half : (i + 1) * half]
            for i in range(3)
            for x in (three_low, three_high)
        ],
        axis=1,
    )
    small_one = lax.dynamic_slice_in_dim(vector_cols, links.tok * height, height, 0).astype(F32)
    return (
        activations,
        pooled,
        pixel_grad,
        base_grad,
        small_one[:, 0],
        small_one[:, 1],
        grad_qkv,
        grad_out,
        small_two[:, 0],
        small_two[:, 1],
        grad_up,
        small_two[:, 2 : 2 + fold].reshape(tall),
        down,
    )


def solution(mesh):
    placed = (
        P("tok", None, None, None),
        P("tok", None),
        P(None, "pix", None),
        P("pix", None),
        P(),
        P(),
        P(),
        P(),
        P(),
        P(),
        P(),
        P(),
        P(),
        P("tok", "pix", None, None),
        P("tok", "pix", None),
    )
    return jax.shard_map(
        local,
        mesh=mesh,
        in_specs=placed,
        out_specs=(
            P("tok", "pix", None, None),
            P("tok", "pix", None),
            P("tok", "pix", None, None),
            P(None, "pix", None),
            P(("pix", "tok")),
            P(("pix", "tok")),
            P(("pix", "tok"), None),
            P(("pix", "tok"), None),
            P(("pix", "tok")),
            P(("pix", "tok")),
            P(("pix", "tok"), None),
            P(("pix", "tok")),
            P(("pix", "tok"), None),
        ),
        check_vma=False,
    )
```

```python
import functools

import jax
import jax.numpy as jnp
from jax import lax
from jax.experimental import pallas as pl
from jax.experimental.pallas import tpu as pltpu
from jax.sharding import PartitionSpec as P

HD = 64
EPSILON = 1e-06
LOG2E = 1.4426950408889634
LN2 = 0.6931471805599453
ROWS = 256
CHUNK = 512
FF_STEP = 256
MIB = 1 << 20
BF = jnp.bfloat16
F32 = jnp.float32


def mm(lhs, rhs, lhs_dim, rhs_dim):
    return lax.dot_general(
        lhs, rhs, (((lhs_dim,), (rhs_dim,)), ((), ())), preferred_element_type=F32
    )


def call(body, grid, prefetch, in_specs, out_specs, out_shape, args, flops, scratch=(), vmem=40, aliases=None):
    moved = sum(a.size * a.dtype.itemsize for a in args)
    moved += sum(o.size * o.dtype.itemsize for o in jax.tree.leaves(out_shape))
    return pl.pallas_call(
        body,
        grid_spec=pltpu.PrefetchScalarGridSpec(
            num_scalar_prefetch=len(prefetch),
            grid=grid,
            in_specs=in_specs,
            out_specs=out_specs,
            scratch_shapes=list(scratch),
        ),
        out_shape=out_shape,
        compiler_params=pltpu.CompilerParams(
            dimension_semantics=("arbitrary",) * len(grid), vmem_limit_bytes=vmem * MIB
        ),
        input_output_aliases=aliases or {},
        cost_estimate=pl.CostEstimate(
            flops=int(flops), bytes_accessed=int(moved), transcendentals=0
        ),
    )(*prefetch, *args)


def shape(dims, dtype):
    return jax.ShapeDtypeStruct(dims, dtype)


def fixed(dims):
    zeros = (0,) * len(dims)
    return pl.BlockSpec(dims, lambda *a: zeros, pipeline_mode=pl.Buffered(1))


def row_stats(x):
    mean = jnp.mean(x, axis=-1, keepdims=True)
    centered = x - mean
    var = jnp.mean(centered * centered, axis=-1, keepdims=True)
    scale = lax.rsqrt(var + EPSILON)
    return centered * scale, scale


def norm_back(grad, normal, scale, gain):
    e = grad * gain
    mean_e = jnp.mean(e, axis=-1, keepdims=True)
    mean_en = jnp.mean(e * normal, axis=-1, keepdims=True)
    return scale * (e - mean_e - normal * mean_en)


def usable_rows(rows, length):
    start = pl.program_id(0) * rows
    index = lax.broadcasted_iota(jnp.int32, (rows, 1), 0) + start
    return (index < length).astype(F32)


def partial_body(info, resize, base, out):
    out[...] = mm(resize[...], base[0], 0, 0).astype(BF)


def partial_kernel(info, resize, base):
    channels, pixels, width = base.shape
    patch = resize.shape[1]
    half = width // 2
    return call(
        partial_body,
        (channels,),
        (info,),
        [
            fixed((pixels, patch)),
            pl.BlockSpec((1, pixels, half), lambda c, s: (c, 0, s[1])),
        ],
        pl.BlockSpec((patch, half), lambda c, s: (c, 0)),
        shape((channels * patch, half), BF),
        (resize, base),
        2 * channels * pixels * patch * half,
    )


def cot_body(info, cot_act, cot_pool, w_down, *outs):
    length = info[2]
    live = usable_rows(cot_act.shape[2], length)
    pooled = cot_pool[...] / length.astype(F32)
    value = ((cot_act[0, 0].astype(F32) + pooled) * live).astype(BF)
    if len(outs) > 1:
        outs[0][...] = value
    outs[-1][...] = mm(value, w_down[...], 1, 1).astype(BF)


def cot_branch(info, cot_act, cot_pool, w_down, part):
    rows, width = cot_act.shape[2:]
    hidden = w_down.shape[0] // 2
    narrow = pl.BlockSpec((ROWS, width), lambda i, s: (i, 0))
    wide = pl.BlockSpec((ROWS, hidden), lambda i, s: (i, 0))
    lead = part == 0
    return call(
        cot_body,
        (rows // ROWS,),
        (info,),
        [
            pl.BlockSpec((1, 1, ROWS, width), lambda i, s: (0, 0, i, 0)),
            fixed((1, width)),
            pl.BlockSpec((hidden, width), lambda i, s: (part, 0), pipeline_mode=pl.Buffered(1)),
        ],
        [narrow, wide] if lead else [wide],
        ([shape((rows, width), BF)] if lead else []) + [shape((rows, hidden), BF)],
        (cot_act, cot_pool, w_down),
        2 * rows * width * hidden,
    )


def embed_body(info, pixels, kernel, gain, shift, w_qkv, embedded, normed, qkv):
    width = embedded.shape[1]
    value = mm(pixels[0, 0], kernel[...], 1, 0).astype(BF)
    embedded[...] = value
    normal, _ = row_stats(value.astype(F32))
    low = (normal * gain[...] + shift[...]).astype(BF)
    normed[...] = low
    for part in range(3):
        cols = slice(part * width, (part + 1) * width)
        product = mm(low, w_qkv[:, cols], 1, 0)
        if part == 0:
            product = product * (HD**-0.5 * LOG2E)
        qkv[:, cols] = product.astype(BF)


def embed_rows(info, pixels, kernel, gain, shift, w_qkv):
    rows, patch = pixels.shape[2:]
    width, triple = w_qkv.shape
    return call(
        embed_body,
        (rows // ROWS,),
        (info,),
        [
            pl.BlockSpec((1, 1, ROWS, patch), lambda i, s: (0, s[0], i, 0)),
            fixed((patch, width)),
            fixed((1, width)),
            fixed((1, width)),
            fixed((width, triple)),
        ],
        [
            pl.BlockSpec((ROWS, width), lambda i, s: (i, 0)),
            pl.BlockSpec((ROWS, width), lambda i, s: (i, 0)),
            pl.BlockSpec((ROWS, triple), lambda i, s: (i, 0)),
        ],
        [shape((rows, width), BF), shape((rows, width), BF), shape((rows, triple), BF)],
        (pixels, kernel, gain, shift, w_qkv),
        2 * rows * width * (patch + triple),
    )


def attend_heads(exact, q_t, k, v_t, extra, probs, inverse, mixed_t):
    rows = k.shape[0]
    lane = lax.broadcasted_iota(jnp.int32, (1, 2 * HD), 1)
    first_row = lax.broadcasted_iota(jnp.int32, (HD, rows), 0) == 0
    ones = jnp.where(first_row, 1.0, 0.0).astype(BF)
    sides = []
    for head in range(2):
        own = slice(head * HD, (head + 1) * HD)
        chosen = jnp.where((lane >= HD) == (head == 1), 1.0, 0.0).astype(BF)
        stack = [q_t[own], ones] if head == 0 else [ones, q_t[own]]
        sides.append((k[...] * chosen + extra[head], jnp.concatenate(stack, axis=0)))
    steps = [(head, start) for head in range(2) for start in range(0, rows, CHUNK)]

    def score(step):
        head, start = step
        return mm(sides[head][0], sides[head][1][:, start : start + CHUNK], 1, 0)

    coming = score(steps[0])
    for n, (head, start) in enumerate(steps):
        own = slice(head * HD, (head + 1) * HD)
        cols = slice(start, start + CHUNK)
        scores = coming
        if n + 1 < len(steps):
            coming = score(steps[n + 1])
        if exact:
            scores = scores - jnp.max(scores, axis=0, keepdims=True)
        power = jnp.exp2(scores)
        total = 1.0 / jnp.sum(power, axis=0, keepdims=True)
        low = power.astype(BF)
        probs[head, :, cols] = low
        inverse[0, head : head + 1, cols] = total
        mixed_t[own, cols] = mm(v_t[own], low, 1, 0) * total


def attend_body(q, k, v, extra, probs, mixed, inverse, mixed_t):
    q_t = q[...].T
    v_t = v[...].T

    def longest(x_t, head):
        square = jnp.square(x_t[head * HD : (head + 1) * HD].astype(F32))
        return jnp.max(jnp.sum(square, axis=0, keepdims=True))

    k_t = k[...].T
    plain = jnp.logical_and(
        longest(q_t, 0) * longest(k_t, 0) <= 3600.0, longest(q_t, 1) * longest(k_t, 1) <= 3600.0
    )
    args = (q_t, k, v_t, extra, probs, inverse, mixed_t)

    @pl.when(plain)
    def _():
        attend_heads(False, *args)

    @pl.when(jnp.logical_not(plain))
    def _():
        attend_heads(True, *args)

    mixed[...] = mixed_t[...].T.astype(BF)


def attend(qkv, extra):
    rows, triple = qkv.shape
    width = triple // 3
    pairs = width // (2 * HD)
    return call(
        attend_body,
        (pairs,),
        (),
        [
            pl.BlockSpec((rows, 2 * HD), lambda j: (0, j)),
            pl.BlockSpec((rows, 2 * HD), lambda j: (0, pairs + j)),
            pl.BlockSpec((rows, 2 * HD), lambda j: (0, 2 * pairs + j)),
            fixed((2, rows, 2 * HD)),
        ],
        [
            pl.BlockSpec((2, rows, rows), lambda j: (j, 0, 0)),
            pl.BlockSpec((rows, 2 * HD), lambda j: (0, j)),
            pl.BlockSpec((1, 2, rows), lambda j: (j, 0, 0)),
        ],
        [
            shape((2 * pairs, rows, rows), BF),
            shape((rows, width), BF),
            shape((pairs, 2, rows), F32),
        ],
        (qkv, qkv, qkv, extra),
        2 * 2 * rows * rows * 256 * 2 * pairs,
        scratch=[pltpu.VMEM((2 * HD, rows), F32)],
    )


def attend_back_body(probs, q, k, v, grad, mixed, inverse, *refs):
    out, dq_t, score_grad = refs[-3:]
    rows = q.shape[0]
    lane = lax.broadcasted_iota(jnp.int32, (1, 2 * HD), 1)
    index = lax.broadcasted_iota(jnp.int32, (HD, rows), 0)
    grad_t = grad[...].T.astype(F32)
    mixed_t = mixed[...].T.astype(F32)
    k_t = k[...].T
    scaled = []
    sides = []
    for head in range(2):
        own = slice(head * HD, (head + 1) * HD)
        total = inverse[0, head : head + 1, :]
        scaled.append((grad_t[own] * total).astype(BF))
        inner = -jnp.sum(grad_t[own] * mixed_t[own], axis=0, keepdims=True) * total
        high = inner.astype(BF).astype(F32)
        sides.append(
            jnp.where(index == 0, high, jnp.where(index == 1, inner - high, 0.0)).astype(BF)
        )
    grad_low = jnp.concatenate(scaled, axis=0).T
    dk_sum = None
    dv_sum = None
    own_lanes = []
    factors = []
    for head in range(2):
        other = (1 - head) * HD
        chosen = jnp.where((lane >= HD) == (head == 1), 1.0, 0.0).astype(BF)
        units = jnp.where((lane == other) | (lane == other + 1), 1.0, 0.0).astype(BF)
        stack = [scaled[0], sides[0]] if head == 0 else [sides[1], scaled[1]]
        own_lanes.append(chosen)
        factors.append((v[...] * chosen + units, jnp.concatenate(stack, axis=0)))
    steps = [(head, start) for head in range(2) for start in range(0, rows, CHUNK)]

    def prob_grad(step):
        head, start = step
        return mm(factors[head][0], factors[head][1][:, start : start + CHUNK], 1, 0)

    coming = prob_grad(steps[0])
    for n, (head, start) in enumerate(steps):
        own = slice(head * HD, (head + 1) * HD)
        cols = slice(start, start + CHUNK)
        shifted = coming
        if n + 1 < len(steps):
            coming = prob_grad(steps[n + 1])
        low = (probs[head, :, cols].astype(F32) * shifted).astype(BF)
        score_grad[:, cols] = low
        dq_t[own, cols] = mm(k_t[own], low, 1, 0)
        if start + CHUNK == rows:
            dv_part = mm(probs[head], grad_low * own_lanes[head], 1, 0)
            dk_part = mm(score_grad[...], q[...] * own_lanes[head], 1, 0)
            dv_sum = dv_part if dv_sum is None else dv_sum + dv_part
            dk_sum = dk_part if dk_sum is None else dk_sum + dk_part
    pair = 2 * HD
    out[:, :pair] = (dq_t[...] * (HD**-0.5)).T.astype(BF)
    out[:, pair : 2 * pair] = (dk_sum * LN2).astype(BF)
    out[:, 2 * pair :] = dv_sum.astype(BF)


def attend_back(probs, qkv, grad_mixed, mixed, inverse, first, pairs, before):
    rows, triple = qkv.shape
    width = triple // 3
    every = width // (2 * HD)

    def column(offset):
        return pl.BlockSpec((rows, 2 * HD), lambda j: (0, offset + j))

    args = (probs, qkv, qkv, qkv, grad_mixed, mixed, inverse)
    specs = [
        pl.BlockSpec((2, rows, rows), lambda j: (first + j, 0, 0)),
        column(first),
        column(every + first),
        column(2 * every + first),
        column(first),
        column(first),
        pl.BlockSpec((1, 2, rows), lambda j: (first + j, 0, 0)),
    ]
    aliases = {}
    if before is not None:
        aliases = {len(args): 0}
        args += (before,)
        specs.append(pl.BlockSpec(memory_space=pl.ANY))
    return call(
        attend_back_body,
        (pairs,),
        (),
        specs,
        pl.BlockSpec((rows, 6 * HD), lambda j: (0, first + j)),
        shape((rows, triple), BF),
        args,
        4 * 2 * rows * rows * 256 * 2 * pairs,
        scratch=[pltpu.VMEM((2 * HD, rows), F32), pltpu.VMEM((rows, rows), BF)],
        aliases=aliases,
    )


def gelu_parts(x):
    size = jnp.abs(x)
    t = 1.0 / (1.0 + (0.3275911 * 0.7071067811865476) * size)
    bell = jnp.exp2((-0.5 * LOG2E) * x * x)
    series = t * (
        0.127414796
        + t * (-0.142248368 + t * (0.7107068705 + t * (-0.7265760135 + t * 0.5307027145)))
    )
    tail = series * bell
    below = jnp.where(x > 0, 1.0 - tail, tail)
    return x * below, below + x * (bell * 0.3989422804014327)


def middle_body(
    info,
    mixed,
    embedded,
    grad_gelu_low,
    grad_gelu_high,
    cot_act,
    cot_pool,
    w_out,
    gain,
    shift,
    w_up,
    b_up,
    middle,
    normed,
    gelu_out,
    grad_pre,
    grad_middle,
    grad_attn,
    grad_mixed,
    sums,
    bias_sum,
):
    rows, width = middle.shape
    hidden = w_up.shape[1]
    step = FF_STEP

    @pl.when(pl.program_id(0) == 0)
    def _():
        sums[...] = jnp.zeros_like(sums)
        bias_sum[...] = jnp.zeros_like(bias_sum)

    value = embedded[...].astype(F32) + mm(mixed[...], w_out[...], 1, 0)
    middle[...] = value
    normal, scale = row_stats(value)
    low = (normal * gain[...] + shift[...]).astype(BF)
    normed[...] = low
    grad_normed = None
    done = None
    coming = mm(low, w_up[:, :step], 1, 0)
    for start in range(0, hidden, step):
        cols = slice(start, start + step)
        pre = coming + b_up[:, cols]
        after = start + step
        if after < hidden:
            coming = mm(low, w_up[:, after : after + step], 1, 0)
        if done is not None:
            grad_normed = done if grad_normed is None else grad_normed + done
        out, slope = gelu_parts(pre)
        gelu_out[:, cols] = out.astype(BF)
        if after <= hidden // 2:
            grad_out = grad_gelu_low[:, cols]
        else:
            grad_out = grad_gelu_high[:, start - hidden // 2 : after - hidden // 2]
        back = (grad_out.astype(F32) * slope).astype(BF)
        grad_pre[:, cols] = back
        bias_sum[:, cols] += jnp.sum(back.astype(F32), axis=0, keepdims=True)
        done = mm(back, w_up[:, cols], 1, 1)
    grad_normed = grad_normed + done
    sums[0:1, :] += jnp.sum(grad_normed * normal, axis=0, keepdims=True)
    sums[1:2, :] += jnp.sum(grad_normed, axis=0, keepdims=True)
    length = info[2]
    live = usable_rows(rows, length)
    pooled = cot_pool[...] / length.astype(F32)
    final = (cot_act[0, 0].astype(F32) + pooled) * live
    total = final + norm_back(grad_normed, normal, scale, gain[...])
    grad_middle[...] = total
    total_low = total.astype(BF)
    grad_attn[...] = total_low
    grad_mixed[...] = mm(total_low, w_out[...], 1, 1).astype(BF)


def middle_rows(
    info, mixed, embedded, low, high, cot_act, cot_pool, w_out, gain, shift, w_up, b_up
):
    rows, width = mixed.shape
    hidden = w_up.shape[1]
    narrow = pl.BlockSpec((ROWS, width), lambda i, s: (i, 0))
    wide = pl.BlockSpec((ROWS, hidden), lambda i, s: (i, 0))
    part = pl.BlockSpec((ROWS, hidden // 2), lambda i, s: (i, 0))
    return call(
        middle_body,
        (rows // ROWS,),
        (info,),
        [
            narrow,
            narrow,
            part,
            part,
            pl.BlockSpec((1, 1, ROWS, width), lambda i, s: (0, 0, i, 0)),
            fixed((1, width)),
            fixed((width, width)),
            fixed((1, width)),
            fixed((1, width)),
            fixed((width, hidden)),
            fixed((1, hidden)),
        ],
        [narrow, narrow, wide, wide, narrow, narrow, narrow]
        + [
            pl.BlockSpec((8, width), lambda i, s: (0, 0)),
            pl.BlockSpec((1, hidden), lambda i, s: (0, 0)),
        ],
        [
            shape((rows, width), F32),
            shape((rows, width), BF),
            shape((rows, hidden), BF),
            shape((rows, hidden), BF),
            shape((rows, width), F32),
            shape((rows, width), BF),
            shape((rows, width), BF),
            shape((8, width), F32),
            shape((1, hidden), F32),
        ],
        (mixed, embedded, low, high, cot_act, cot_pool, w_out, gain, shift, w_up, b_up),
        2 * rows * width * (2 * width + 2 * hidden),
    )


SAME_QUARTER = (3, 1, 2, 0)


def down_body(order, which, left, right_theirs, right_mine, theirs, mine):
    half = right_mine.shape[1]
    both = jnp.concatenate([right_theirs[...], right_mine[...]], axis=1)
    out = mm(left[...], both, 0, 0)
    theirs[0] = out[:, :half].astype(BF)
    mine[0] = out[:, half:].astype(BF)


def grad_down_halves(order, which, gelu_out, branch, first, count):
    rows, hidden = gelu_out.shape
    half = branch.shape[1] // 2
    tall = hidden // 4
    block = (1, tall, half)
    return call(
        down_body,
        (count,),
        (order, which),
        [
            pl.BlockSpec((rows, tall), lambda j, o, w: (0, o[first + j])),
            pl.BlockSpec((rows, half), lambda j, o, w: (0, 1 - w[0])),
            pl.BlockSpec((rows, half), lambda j, o, w: (0, w[0])),
        ],
        [
            pl.BlockSpec(block, lambda j, o, w: (j, 0, 0)),
            pl.BlockSpec(block, lambda j, o, w: (j, 0, 0)),
        ],
        [shape((count, tall, half), BF)] * 2,
        (gelu_out, branch, branch),
        rows * hidden * half * count,
    )


def place_quarters(places, value, theirs, mine, rows=None):
    quarter = value.shape[0] // 4
    lanes = mine.shape[2]
    for i in range(4):
        block = value[i * quarter : (i + 1) * quarter].astype(BF)
        theirs[places[4 + i], :quarter, :] = block[:, :lanes]
        mine[places[i], :quarter, :] = block[:, lanes:]


def up_body(
    places, which, normed, pre_theirs, pre_mine, mixed, attn_theirs, attn_mine, theirs, mine
):
    step = pl.program_id(0)
    last = pl.num_programs(0) - 1

    @pl.when(step < last)
    def _():
        both = jnp.concatenate([pre_theirs[...], pre_mine[...]], axis=1)
        place_quarters(places, mm(normed[...], both, 0, 0), theirs, mine)

    @pl.when(step == last)
    def _():
        both = jnp.concatenate([attn_theirs[...], attn_mine[...]], axis=1)
        place_quarters(places, mm(mixed[...], both, 0, 0), theirs, mine)


def column_call(body, order, which, grid, lanes, quarter, specs, args, flops):
    total = grid * lanes
    return call(
        body,
        (grid,),
        (order, which),
        specs,
        [pl.BlockSpec((4, quarter, lanes), lambda j, o, w: (0, 0, j))] * 2,
        [shape((4, quarter, total), BF)] * 2,
        args,
        flops,
    )


def grad_up_halves(order, which, normed, grad_pre, mixed, grad_attn):
    rows, width = normed.shape
    half = width // 2
    lanes = half
    steps = grad_pre.shape[1] // 2 // lanes

    def hidden_block(core):
        return pl.BlockSpec(
            (rows, lanes), lambda j, o, w: (0, core(w) * steps + jnp.minimum(j, steps - 1))
        )

    specs = [
        fixed((rows, width)),
        hidden_block(lambda w: 1 - w[0]),
        hidden_block(lambda w: w[0]),
        fixed((rows, width)),
        pl.BlockSpec((rows, half), lambda j, o, w: (0, 1 - w[0])),
        pl.BlockSpec((rows, half), lambda j, o, w: (0, w[0])),
    ]
    return column_call(
        up_body,
        order,
        which,
        steps + 1,
        lanes,
        width // 4,
        specs,
        (normed, grad_pre, grad_pre, mixed, grad_attn, grad_attn),
        4 * rows * width * (steps * lanes + half),
    )


def qkv_body(places, which, normed, grad_theirs, grad_mine, theirs, mine):
    both = jnp.concatenate([grad_theirs[...], grad_mine[...]], axis=1)
    place_quarters(places, mm(normed[...], both, 0, 0), theirs, mine)


def grad_qkv_halves(order, which, normed, grad_qkv):
    rows, width = normed.shape
    steps = 3
    lanes = grad_qkv.shape[1] // 2 // steps
    specs = [
        fixed((rows, width)),
        pl.BlockSpec((rows, lanes), lambda j, o, w: (0, (1 - w[0]) * steps + j)),
        pl.BlockSpec((rows, lanes), lambda j, o, w: (0, w[0] * steps + j)),
    ]
    return column_call(
        qkv_body,
        order,
        which,
        steps,
        lanes,
        width // 4,
        specs,
        (normed, grad_qkv, grad_qkv),
        4 * rows * width * steps * lanes,
    )


def kernel_body(
    places, which, pixels, grad_theirs, grad_mine, sums_one, sums_two, bias, theirs, mine
):
    both = jnp.concatenate([grad_theirs[...], grad_mine[...]], axis=1)
    out = mm(pixels[0, 0], both, 0, 0)
    place_quarters(places, out, theirs, mine)
    quarter = out.shape[0] // 4
    lanes = mine.shape[2]
    width = sums_one.shape[1] // 4
    folds = bias.shape[1] // 4 // width
    for i in range(4):
        cols = slice(i * width, (i + 1) * width)
        rows = [sums_one[0:1, cols], sums_one[1:2, cols], sums_two[0:1, cols], sums_two[1:2, cols]]
        for n in range(folds):
            at = (i * folds + n) * width
            rows.append(bias[:, at : at + width])
        rows.append(jnp.zeros((16 - len(rows), width), F32))
        block = jnp.concatenate(
            [jnp.concatenate(rows, axis=0), jnp.zeros((16, lanes - width), F32)], axis=1
        ).astype(BF)
        theirs[places[4 + i], quarter:, :] = block
        mine[places[i], quarter:, :] = block


def grad_kernel_halves(order, which, pixels, grad, sums_one, sums_two, bias):
    rows, patch = pixels.shape[2:]
    half = grad.shape[1] // 2
    specs = [
        pl.BlockSpec((1, 1, rows, patch), lambda j, o, w: (0, w[1], 0, 0)),
        pl.BlockSpec((rows, half), lambda j, o, w: (0, 1 - w[0])),
        pl.BlockSpec((rows, half), lambda j, o, w: (0, w[0])),
        fixed(sums_one.shape),
        fixed(sums_two.shape),
        fixed(bias.shape),
    ]
    return column_call(
        kernel_body,
        order,
        which,
        1,
        half,
        patch // 4 + 16,
        specs,
        (pixels, grad, grad, sums_one, sums_two, bias),
        4 * rows * patch * half,
    )


def first_back_body(grad_qkv, w_qkv, embedded, gain, grad_middle, out, sums):
    width = out.shape[1]
    pair = 2 * HD

    @pl.when(pl.program_id(0) == 0)
    def _():
        sums[...] = jnp.zeros_like(sums)

    grad = None
    for i in range(3):
        starts = range(i * pair, 3 * width, 3 * pair)
        value = jnp.concatenate([grad_qkv[:, at : at + pair] for at in starts], axis=1)
        part = mm(value, w_qkv[:, i * width : (i + 1) * width], 1, 1)
        grad = part if grad is None else grad + part
    normal, scale = row_stats(embedded[...].astype(F32))
    sums[0:1, :] += jnp.sum(grad * normal, axis=0, keepdims=True)
    sums[1:2, :] += jnp.sum(grad, axis=0, keepdims=True)
    out[...] = (grad_middle[...] + norm_back(grad, normal, scale, gain[...])).astype(BF)


def first_back(grad_qkv, w_qkv, embedded, gain, grad_middle):
    rows, width = embedded.shape
    narrow = pl.BlockSpec((ROWS, width), lambda i: (i, 0))
    return call(
        first_back_body,
        (rows // ROWS,),
        (),
        [
            pl.BlockSpec((ROWS, 3 * width), lambda i: (i, 0)),
            fixed(w_qkv.shape),
            narrow,
            fixed((1, width)),
            narrow,
        ],
        [narrow, pl.BlockSpec((8, width), lambda i: (0, 0))],
        [shape((rows, width), BF), shape((8, width), F32)],
        (grad_qkv, w_qkv, embedded, gain, grad_middle),
        2 * rows * width * 3 * width,
    )


def last_body(info, middle, gelu_out, w_down, activations, pooled):
    rows = middle.shape[0]
    length = info[2]

    @pl.when(pl.program_id(0) == 0)
    def _():
        pooled[...] = jnp.zeros_like(pooled)

    final = middle[...] + mm(gelu_out[...], w_down[...], 1, 0)
    final = final * usable_rows(rows, length)
    activations[0, 0] = final.astype(BF)
    pooled[0] += jnp.sum(final, axis=0, keepdims=True)

    @pl.when(pl.program_id(0) == pl.num_programs(0) - 1)
    def _():
        pooled[...] = pooled[...] / length.astype(F32)


def last_rows(info, middle, gelu_out, w_down):
    rows, width = middle.shape
    hidden = w_down.shape[0]
    return call(
        last_body,
        (rows // ROWS,),
        (info,),
        [
            pl.BlockSpec((ROWS, width), lambda i, s: (i, 0)),
            pl.BlockSpec((ROWS, hidden), lambda i, s: (i, 0)),
            fixed((hidden, width)),
        ],
        [
            pl.BlockSpec((1, 1, ROWS, width), lambda i, s: (0, 0, i, 0)),
            pl.BlockSpec((1, 1, width), lambda i, s: (0, 0, 0)),
        ],
        [shape((1, 1, rows, width), BF), shape((1, 1, width), F32)],
        (middle, gelu_out, w_down),
        2 * rows * width * hidden,
    )


def pixel_body(grad_embedded, kernel, pixel_grad):
    pixel_grad[0, 0] = mm(grad_embedded[...], kernel[...], 1, 1)


def pixel_rows(grad_embedded, kernel):
    rows, width = grad_embedded.shape
    patch = kernel.shape[0]
    return call(
        pixel_body,
        (rows // ROWS,),
        (),
        [pl.BlockSpec((ROWS, width), lambda i: (i, 0)), fixed((patch, width))],
        pl.BlockSpec((1, 1, ROWS, patch), lambda i: (0, 0, i, 0)),
        shape((1, 1, rows, patch), F32),
        (grad_embedded, kernel),
        2 * rows * width * patch,
    )


def base_body(order, order_far, which, resize, near, far, out, work):
    half = near.shape[2]
    quarter = near.shape[1]
    patch = resize.shape[1]
    for j in range(4):
        rows = pl.ds(pl.multiple_of(order[j] * quarter, quarter), quarter)
        work[which[0], rows, :] = near[j]
        rows = pl.ds(pl.multiple_of(order_far[j] * quarter, quarter), quarter)
        work[1 - which[0], rows, :] = far[j]
    for c in range(out.shape[0]):
        for h in range(2):
            out[c, :, h * half : (h + 1) * half] = mm(
                resize[...], work[h, c * patch : (c + 1) * patch, :], 1, 0
            )


def base_grad_of(order, order_far, which, resize, near, far, channels):
    pixels, patch = resize.shape
    _, quarter, half = near.shape
    return call(
        base_body,
        (1,),
        (order, order_far, which),
        [fixed(resize.shape), fixed(near.shape), fixed(far.shape)],
        fixed((channels, pixels, 2 * half)),
        shape((channels, pixels, 2 * half), F32),
        (resize, near, far),
        2 * channels * pixels * patch * 2 * half,
        scratch=[pltpu.VMEM((2, 4 * quarter, half), BF)],
    )


class Links:
    def __init__(self):
        self.parts = lax.axis_size("pix")
        self.count = lax.axis_size("tok")
        self.pix = lax.axis_index("pix")
        self.tok = lax.axis_index("tok")
        self.core = self.tok % 2
        self.chips = self.count // 2
        self.near = 1 + self.core
        self.far = 2 - self.core

    def swap(self, value, partner):
        pairs = []
        for p in range(self.parts):
            for t in range(self.count):
                q, u = partner(p, t)
                pairs.append((p * self.count + t, q * self.count + u))
        return lax.ppermute(value, ("pix", "tok"), pairs)

    def core_swap(self, value):
        return self.swap(value, lambda p, t: (p, t ^ 1))

    def first_swap(self, value):
        return self.swap(value, lambda p, t: (p ^ (1 + t % 2), t))

    def second_swap(self, value):
        return self.swap(value, lambda p, t: (p ^ (2 - t % 2), t))

    def chip_swap(self, value, bit):
        return self.swap(value, lambda p, t: (p, t ^ (2 << bit)))

    def quarters(self, near, far):
        pix = self.pix
        return jnp.stack([pix ^ near, pix ^ 3, pix, pix ^ far]).astype(jnp.int32)


def places_of(order):
    return jnp.argmax(order[None, :] == jnp.arange(4)[:, None], axis=1).astype(jnp.int32)


def together(*values):
    return lax.optimization_barrier(values)


def add(a, b, dtype=BF):
    return (a.astype(F32) + b.astype(F32)).astype(dtype)


def combine(arrived, mine):
    return add(arrived[:2], mine[:2]), add(arrived[2:], mine[2:])


class Order:
    def __init__(self):
        self.last = ()

    def __call__(self, work, *values):
        flat, tree = jax.tree.flatten(values)
        count = len(flat)
        if self.last:
            flat = list(together(*flat, *self.last))[:count]
        result = work(*jax.tree.unflatten(tree, flat))
        self.last = tuple(jax.tree.leaves(result))
        return result


class Chain:
    def __init__(self, order, links, away, keep, height):
        self.order, self.links, self.height = order, links, height
        self.stage = 0
        self.last = 1 + links.chips.bit_length() - 1
        self.arrived = links.first_swap(away)
        self.staying = keep

    def advance(self):
        links, stage = self.links, self.stage
        if stage > self.last:
            return

        def quarters(arrived, staying):
            return add(arrived[1], staying[1]), add(arrived[0], staying[0])

        def split(value, bit):
            own = (links.tok >> (bit + 1)) & 1
            value = value.reshape(value.shape[0] // 2, 2, *value.shape[1:])
            leaving = lax.dynamic_index_in_dim(value, 1 - own, 1, keepdims=False)
            return leaving, lax.dynamic_index_in_dim(value, own, 1, keepdims=False)

        def pix_sum(arrived, staying):
            value = add(arrived, staying)
            return split(value.reshape(links.chips, self.height, -1), 0)

        def chip_sum(arrived, staying):
            return split(add(arrived, staying), stage - 1)

        def last_sum(arrived, staying):
            return add(arrived, staying, F32).reshape(self.height, -1)

        work = quarters if stage == 0 else pix_sum if stage == 1 else chip_sum
        if stage == self.last:
            self.value = self.order(last_sum, self.arrived, self.staying)
        else:
            leaving, self.staying = self.order(work, self.arrived, self.staying)
            if stage == 0:
                self.arrived = links.second_swap(leaving)
            else:
                self.arrived = links.chip_swap(leaving, stage - 1)
        self.stage += 1

    def finish(self):
        while self.stage <= self.last:
            self.advance()
        return self.value


def own_rows(links, block):
    pair = block.reshape(2, block.shape[0] // 2, block.shape[1])
    mine = lax.dynamic_index_in_dim(pair, links.core, 0, keepdims=False)
    arrived = links.core_swap(
        lax.dynamic_index_in_dim(pair, 1 - links.core, 0, keepdims=False)
    )
    first = links.core == 0
    return jnp.where(first, mine, arrived), jnp.where(first, arrived, mine)


def local(
    pixels,
    lengths,
    base_kernel,
    resize,
    gain_one,
    shift_one,
    w_qkv,
    w_out,
    gain_two,
    shift_two,
    w_up,
    b_up,
    w_down,
    cot_act,
    cot_pool,
):
    links = Links()
    turn = Order()
    seq_len = pixels.shape[2]
    width = w_qkv.shape[0]
    hidden = w_up.shape[1]
    channels = base_kernel.shape[0]
    half = width // 2
    core = links.core
    own_length = lax.dynamic_index_in_dim(lengths[0], links.pix, 0, keepdims=False)
    info = jnp.stack([links.pix, core, own_length]).astype(jnp.int32)
    mine = jnp.stack([core, links.pix]).astype(jnp.int32)
    order = links.quarters(links.near, links.far)
    order_theirs = links.quarters(links.far, links.near)
    places = jnp.concatenate([places_of(order), places_of(order_theirs)])
    gain_one, shift_one = gain_one[None], shift_one[None]
    gain_two, shift_two, b_up = gain_two[None], shift_two[None], b_up[None]
    cot_pool = cot_pool[0]

    piece = partial_kernel(info, resize, base_kernel)
    piece = add(links.first_swap(piece), piece)
    branch, gelu_low = cot_branch(info, cot_act, cot_pool, w_down, 0)
    piece, branch, gelu_low = together(piece, branch, gelu_low)
    piece = add(links.second_swap(piece), piece)
    (gelu_high,) = cot_branch(info, cot_act, cot_pool, w_down, 1)
    piece, gelu_high = together(piece, gelu_high)
    other = links.core_swap(piece)
    kernel = jnp.concatenate(
        [jnp.where(core == 0, piece, other), jnp.where(core == 0, other, piece)], axis=1
    )

    lane = jnp.arange(2 * HD)[None, None, :]
    slot = jnp.array([HD, 0])[:, None, None]
    blocked = (jnp.arange(seq_len) >= own_length)[None, :, None] & (lane == slot)
    extra = jnp.where(blocked, -1e30, 0.0).astype(BF)

    embedded, normed, qkv = embed_rows(info, pixels, kernel, gain_one, shift_one, w_qkv)
    probs, mixed, inverse = attend(qkv, extra)
    (
        middle,
        normed_two,
        gelu_out,
        grad_pre,
        grad_middle,
        grad_attn,
        grad_mixed,
        sums_two,
        bias_sum,
    ) = middle_rows(
        info,
        mixed,
        embedded,
        gelu_low,
        gelu_high,
        cot_act,
        cot_pool,
        w_out,
        gain_two,
        shift_two,
        w_up,
        b_up,
    )

    blocks = links.parts * links.chips
    up_theirs, up_mine = turn(
        lambda *a: grad_up_halves(places, mine, *a), normed_two, grad_pre, mixed, grad_attn
    )
    up_arrived = links.core_swap(up_theirs)
    away_theirs, away_mine = turn(
        lambda *a: grad_down_halves(order, mine, *a, 0, 2), gelu_out, branch
    )
    away_arrived = links.core_swap(away_theirs)
    up_arrived, gelu_last = together(up_arrived, gelu_out)
    keep_theirs, keep_mine = turn(
        lambda *a: grad_down_halves(order, mine, *a, 2, 2), gelu_last, branch
    )
    keep_arrived = links.core_swap(keep_theirs)
    up_away, up_keep = turn(combine, up_arrived, up_mine)
    up = Chain(turn, links, up_away, up_keep, width // blocks)

    def combine_down(away_arrived, away_mine, keep_arrived, keep_mine):
        away = add(jnp.stack([keep_arrived[1], away_arrived[1]]), away_mine)
        return away, add(jnp.stack([keep_arrived[0], away_arrived[0]]), keep_mine)

    down_away, down_keep = turn(combine_down, away_arrived, away_mine, keep_arrived, keep_mine)
    down = Chain(turn, links, down_away, down_keep, hidden // blocks)

    every = width // (2 * HD)
    cuts = [every // 3 * n for n in range(3)] + [every]

    def back(n, before):
        return turn(
            lambda probs, *a: attend_back(
                probs, qkv, grad_mixed, mixed, inverse, cuts[n], cuts[n + 1] - cuts[n], *a
            ),
            probs,
            before,
        )

    grad_qkv = back(0, None)
    down.advance()
    grad_qkv = back(1, grad_qkv)
    grad_qkv = back(2, grad_qkv)
    up.advance()
    down.advance()

    grad_embedded, sums_one = turn(
        lambda *a: first_back(*a, w_qkv, embedded, gain_one, grad_middle), grad_qkv
    )
    kernel_theirs, kernel_mine = turn(
        lambda *a: grad_kernel_halves(places, mine, pixels, *a, sums_two, bias_sum),
        grad_embedded,
        sums_one,
    )
    arrived = links.core_swap(kernel_theirs)
    down.advance()
    up.advance()
    away, keep = turn(combine, arrived, kernel_mine)
    arrived = links.first_swap(away)

    three_theirs, three_mine = turn(
        lambda *a: grad_qkv_halves(places, mine, *a), normed, grad_qkv
    )
    three_arrived = links.core_swap(three_theirs)
    leaving, staying = turn(
        lambda a, b: (add(a[1], b[1]), add(a[0], b[0])), arrived, keep
    )
    arrived = links.second_swap(leaving)
    up.advance()
    three_away, three_keep = turn(combine, three_arrived, three_mine)
    quarter = turn(add, arrived, staying)
    arrived = links.chip_swap(quarter, 0)
    three = Chain(turn, links, three_away, three_keep, width // blocks)
    pixel_grad = turn(pixel_rows, grad_embedded, kernel)
    quarter = turn(add, arrived, quarter)
    arrived = links.chip_swap(quarter, 1)
    activations, pooled = turn(
        lambda *a: last_rows(info, *a), middle, gelu_out, w_down
    )
    three.advance()
    quarter = turn(add, arrived, quarter)
    for bit in range(2, links.chips.bit_length() - 1):
        arrived = links.chip_swap(quarter, bit)
        quarter = turn(add, arrived, quarter)
    vectors = quarter[-16:, : width // links.parts].astype(F32)
    quarter = quarter[:-16]
    arrived = links.second_swap(quarter)
    three.advance()
    pair = turn(lambda a, b: jnp.stack([a, b]), quarter, arrived)
    arrived = links.first_swap(pair)
    three.advance()
    full = turn(lambda a, b: jnp.concatenate([a, b], axis=0), arrived, pair)
    arrived = links.core_swap(full)
    three.advance()
    base_grad = turn(
        lambda *a: base_grad_of(order, order_theirs, mine, resize, *a, channels), full, arrived
    )
    up, down, three = up.finish(), down.finish(), three.finish()

    height = width // (links.parts * links.count)
    tall = hidden // (links.parts * links.count)
    down = jnp.concatenate(own_rows(links, down), axis=1)
    up_cols = hidden // 2
    up_low, up_high = own_rows(links, up)
    grad_up = jnp.concatenate([up_low[:, :up_cols], up_high[:, :up_cols]], axis=1)
    out_cols = slice(up_cols, up_cols + half)
    grad_out = jnp.concatenate([up_low[:, out_cols], up_high[:, out_cols]], axis=1)
    three_low, three_high = own_rows(links, three)
    pair = 2 * HD
    pieces = []
    for i in range(3):
        for value in (three_low, three_high):
            for at in range(i * pair, value.shape[1], 3 * pair):
                pieces.append(value[:, at : at + pair])
    grad_qkv = jnp.concatenate(pieces, axis=1)
    small = lax.dynamic_slice_in_dim(vectors[:4], links.tok * height, height, 1)
    folds = hidden // width
    grad_bias = lax.dynamic_slice_in_dim(
        vectors[4 : 4 + folds].reshape(-1), links.tok * tall, tall, 0
    )
    return (
        activations,
        pooled,
        pixel_grad,
        base_grad,
        small[0],
        small[1],
        grad_qkv,
        grad_out,
        small[2],
        small[3],
        grad_up,
        grad_bias,
        down,
    )


def solution(mesh):
    placed = (
        P("tok", None, None, None),
        P("tok", None),
        P(None, "pix", None),
        P("pix", None),
        P(),
        P(),
        P(),
        P(),
        P(),
        P(),
        P(),
        P(),
        P(),
        P("tok", "pix", None, None),
        P("tok", "pix", None),
    )
    return jax.shard_map(
        local,
        mesh=mesh,
        in_specs=placed,
        out_specs=(
            P("tok", "pix", None, None),
            P("tok", "pix", None),
            P("tok", "pix", None, None),
            P(None, "pix", None),
            P(("pix", "tok")),
            P(("pix", "tok")),
            P(("pix", "tok"), None),
            P(("pix", "tok"), None),
            P(("pix", "tok")),
            P(("pix", "tok")),
            P(("pix", "tok"), None),
            P(("pix", "tok")),
            P(("pix", "tok"), None),
        ),
        check_vma=False,
    )
```

```python
import functools

import jax
import jax.numpy as jnp
from jax import lax
from jax.experimental import pallas as pl
from jax.experimental.pallas import tpu as pltpu
from jax.sharding import PartitionSpec as P

HD = 64
EPSILON = 1e-06
LOG2E = 1.4426950408889634
LN2 = 0.6931471805599453
ROWS = 256
CHUNK = 512
FF_STEP = 256
MIB = 1 << 20
BF = jnp.bfloat16
F32 = jnp.float32


def mm(lhs, rhs, lhs_dim, rhs_dim):
    return lax.dot_general(
        lhs, rhs, (((lhs_dim,), (rhs_dim,)), ((), ())), preferred_element_type=F32
    )


def call(body, grid, prefetch, in_specs, out_specs, out_shape, args, flops, scratch=(), vmem=40, aliases=None, light=False):
    moved = sum(a.size * a.dtype.itemsize for a in args)
    moved += sum(o.size * o.dtype.itemsize for o in jax.tree.leaves(out_shape))
    return pl.pallas_call(
        body,
        grid_spec=pltpu.PrefetchScalarGridSpec(
            num_scalar_prefetch=len(prefetch),
            grid=grid,
            in_specs=in_specs,
            out_specs=out_specs,
            scratch_shapes=list(scratch),
        ),
        out_shape=out_shape,
        compiler_params=pltpu.CompilerParams(
            dimension_semantics=("arbitrary",) * len(grid), vmem_limit_bytes=vmem * MIB
        ),
        input_output_aliases=aliases or {},
        cost_estimate=pl.CostEstimate(
            flops=1 if light else int(flops),
            bytes_accessed=1 if light else int(moved),
            transcendentals=0,
        ),
    )(*prefetch, *args)


def shape(dims, dtype):
    return jax.ShapeDtypeStruct(dims, dtype)


def fixed(dims):
    zeros = (0,) * len(dims)
    return pl.BlockSpec(dims, lambda *a: zeros, pipeline_mode=pl.Buffered(1))


def row_stats(x):
    mean = jnp.mean(x, axis=-1, keepdims=True)
    centered = x - mean
    var = jnp.mean(centered * centered, axis=-1, keepdims=True)
    scale = lax.rsqrt(var + EPSILON)
    return centered * scale, scale


def norm_back(grad, normal, scale, gain):
    e = grad * gain
    mean_e = jnp.mean(e, axis=-1, keepdims=True)
    mean_en = jnp.mean(e * normal, axis=-1, keepdims=True)
    return scale * (e - mean_e - normal * mean_en)


def usable_rows(rows, length):
    start = pl.program_id(0) * rows
    index = lax.broadcasted_iota(jnp.int32, (rows, 1), 0) + start
    return (index < length).astype(F32)


def partial_body(resize, base, out):
    half = out.shape[1]
    start = pl.multiple_of(lax.axis_index("tok") % 2 * half, half)
    out[...] = mm(resize[...], base[0, :, pl.ds(start, half)], 0, 0).astype(BF)


def partial_kernel(resize, base):
    channels, pixels, width = base.shape
    patch = resize.shape[1]
    half = width // 2
    return call(
        partial_body,
        (channels,),
        (),
        [fixed((pixels, patch)), pl.BlockSpec((1, pixels, width), lambda c: (c, 0, 0))],
        pl.BlockSpec((patch, half), lambda c: (c, 0)),
        shape((channels * patch, half), BF),
        (resize, base),
        2 * channels * pixels * patch * half,
    )


def cot_body(info, cot_act, cot_pool, w_down, *outs):
    length = info[2]
    live = usable_rows(cot_act.shape[2], length)
    pooled = cot_pool[...] / length.astype(F32)
    value = ((cot_act[0, 0].astype(F32) + pooled) * live).astype(BF)
    if len(outs) > 1:
        outs[0][...] = value
    outs[-1][...] = mm(value, w_down[...], 1, 1).astype(BF)


def cot_branch(info, cot_act, cot_pool, w_down, part):
    rows, width = cot_act.shape[2:]
    hidden = w_down.shape[0] // 2
    narrow = pl.BlockSpec((ROWS, width), lambda i, s: (i, 0))
    wide = pl.BlockSpec((ROWS, hidden), lambda i, s: (i, 0))
    lead = part == 0
    return call(
        cot_body,
        (rows // ROWS,),
        (info,),
        [
            pl.BlockSpec((1, 1, ROWS, width), lambda i, s: (0, 0, i, 0)),
            fixed((1, width)),
            pl.BlockSpec((hidden, width), lambda i, s: (part, 0), pipeline_mode=pl.Buffered(1)),
        ],
        [narrow, wide] if lead else [wide],
        ([shape((rows, width), BF)] if lead else []) + [shape((rows, hidden), BF)],
        (cot_act, cot_pool, w_down),
        2 * rows * width * hidden,
    )


def embed_body(info, pixels, kernel, gain, shift, w_qkv, embedded, normed, qkv):
    width = embedded.shape[1]
    value = mm(pixels[0, 0], kernel[...], 1, 0).astype(BF)
    embedded[...] = value
    normal, _ = row_stats(value.astype(F32))
    low = (normal * gain[...] + shift[...]).astype(BF)
    normed[...] = low
    for part in range(3):
        cols = slice(part * width, (part + 1) * width)
        product = mm(low, w_qkv[:, cols], 1, 0)
        if part == 0:
            product = product * (HD**-0.5 * LOG2E)
        qkv[:, cols] = product.astype(BF)


def embed_rows(info, pixels, kernel, gain, shift, w_qkv):
    rows, patch = pixels.shape[2:]
    width, triple = w_qkv.shape
    return call(
        embed_body,
        (rows // ROWS,),
        (info,),
        [
            pl.BlockSpec((1, 1, ROWS, patch), lambda i, s: (0, s[0], i, 0)),
            fixed((patch, width)),
            fixed((1, width)),
            fixed((1, width)),
            fixed((width, triple)),
        ],
        [
            pl.BlockSpec((ROWS, width), lambda i, s: (i, 0)),
            pl.BlockSpec((ROWS, width), lambda i, s: (i, 0)),
            pl.BlockSpec((ROWS, triple), lambda i, s: (i, 0)),
        ],
        [shape((rows, width), BF), shape((rows, width), BF), shape((rows, triple), BF)],
        (pixels, kernel, gain, shift, w_qkv),
        2 * rows * width * (patch + triple),
    )


def attend_heads(exact, q_t, k, v_t, extra, probs, inverse, mixed_t):
    rows = k.shape[0]
    lane = lax.broadcasted_iota(jnp.int32, (1, 2 * HD), 1)
    first_row = lax.broadcasted_iota(jnp.int32, (HD, rows), 0) == 0
    ones = jnp.where(first_row, 1.0, 0.0).astype(BF)
    sides = []
    for head in range(2):
        own = slice(head * HD, (head + 1) * HD)
        chosen = jnp.where((lane >= HD) == (head == 1), 1.0, 0.0).astype(BF)
        stack = [q_t[own], ones] if head == 0 else [ones, q_t[own]]
        sides.append((k[...] * chosen + extra[head], jnp.concatenate(stack, axis=0)))
    steps = [(head, start) for head in range(2) for start in range(0, rows, CHUNK)]

    def score(step):
        head, start = step
        return mm(sides[head][0], sides[head][1][:, start : start + CHUNK], 1, 0)

    coming = score(steps[0])
    for n, (head, start) in enumerate(steps):
        own = slice(head * HD, (head + 1) * HD)
        cols = slice(start, start + CHUNK)
        scores = coming
        if n + 1 < len(steps):
            coming = score(steps[n + 1])
        if exact:
            scores = scores - jnp.max(scores, axis=0, keepdims=True)
        power = jnp.exp2(scores)
        total = 1.0 / jnp.sum(power, axis=0, keepdims=True)
        low = power.astype(BF)
        probs[head, :, cols] = low
        inverse[0, head : head + 1, cols] = total
        mixed_t[own, cols] = mm(v_t[own], low, 1, 0) * total


def attend_body(q, k, v, extra, probs, mixed, inverse, mixed_t):
    q_t = q[...].T
    v_t = v[...].T

    def longest(x_t, head):
        square = jnp.square(x_t[head * HD : (head + 1) * HD].astype(F32))
        return jnp.max(jnp.sum(square, axis=0, keepdims=True))

    k_t = k[...].T
    plain = jnp.logical_and(
        longest(q_t, 0) * longest(k_t, 0) <= 3600.0, longest(q_t, 1) * longest(k_t, 1) <= 3600.0
    )
    args = (q_t, k, v_t, extra, probs, inverse, mixed_t)

    @pl.when(plain)
    def _():
        attend_heads(False, *args)

    @pl.when(jnp.logical_not(plain))
    def _():
        attend_heads(True, *args)

    mixed[...] = mixed_t[...].T.astype(BF)


def attend(qkv, extra):
    rows, triple = qkv.shape
    width = triple // 3
    pairs = width // (2 * HD)
    return call(
        attend_body,
        (pairs,),
        (),
        [
            pl.BlockSpec((rows, 2 * HD), lambda j: (0, j)),
            pl.BlockSpec((rows, 2 * HD), lambda j: (0, pairs + j)),
            pl.BlockSpec((rows, 2 * HD), lambda j: (0, 2 * pairs + j)),
            fixed((2, rows, 2 * HD)),
        ],
        [
            pl.BlockSpec((2, rows, rows), lambda j: (j, 0, 0)),
            pl.BlockSpec((rows, 2 * HD), lambda j: (0, j)),
            pl.BlockSpec((1, 2, rows), lambda j: (j, 0, 0)),
        ],
        [
            shape((2 * pairs, rows, rows), BF),
            shape((rows, width), BF),
            shape((pairs, 2, rows), F32),
        ],
        (qkv, qkv, qkv, extra),
        2 * 2 * rows * rows * 256 * 2 * pairs,
        scratch=[pltpu.VMEM((2 * HD, rows), F32)],
    )


def attend_back_body(probs, q, k, v, grad, mixed, inverse, *refs):
    out, dq_t, score_grad = refs[-3:]
    rows = q.shape[0]
    lane = lax.broadcasted_iota(jnp.int32, (1, 2 * HD), 1)
    index = lax.broadcasted_iota(jnp.int32, (HD, rows), 0)
    grad_t = grad[...].T.astype(F32)
    mixed_t = mixed[...].T.astype(F32)
    k_t = k[...].T
    scaled = []
    sides = []
    for head in range(2):
        own = slice(head * HD, (head + 1) * HD)
        total = inverse[0, head : head + 1, :]
        scaled.append((grad_t[own] * total).astype(BF))
        inner = -jnp.sum(grad_t[own] * mixed_t[own], axis=0, keepdims=True) * total
        high = inner.astype(BF).astype(F32)
        sides.append(
            jnp.where(index == 0, high, jnp.where(index == 1, inner - high, 0.0)).astype(BF)
        )
    grad_low = jnp.concatenate(scaled, axis=0).T
    dk_sum = None
    dv_sum = None
    own_lanes = []
    factors = []
    for head in range(2):
        other = (1 - head) * HD
        chosen = jnp.where((lane >= HD) == (head == 1), 1.0, 0.0).astype(BF)
        units = jnp.where((lane == other) | (lane == other + 1), 1.0, 0.0).astype(BF)
        stack = [scaled[0], sides[0]] if head == 0 else [sides[1], scaled[1]]
        own_lanes.append(chosen)
        factors.append((v[...] * chosen + units, jnp.concatenate(stack, axis=0)))
    steps = [(head, start) for head in range(2) for start in range(0, rows, CHUNK)]

    def prob_grad(step):
        head, start = step
        return mm(factors[head][0], factors[head][1][:, start : start + CHUNK], 1, 0)

    coming = prob_grad(steps[0])
    for n, (head, start) in enumerate(steps):
        own = slice(head * HD, (head + 1) * HD)
        cols = slice(start, start + CHUNK)
        shifted = coming
        if n + 1 < len(steps):
            coming = prob_grad(steps[n + 1])
        low = (probs[head, :, cols].astype(F32) * shifted).astype(BF)
        score_grad[:, cols] = low
        dq_t[own, cols] = mm(k_t[own], low, 1, 0)
        if start + CHUNK == rows:
            dv_part = mm(probs[head], grad_low * own_lanes[head], 1, 0)
            dk_part = mm(score_grad[...], q[...] * own_lanes[head], 1, 0)
            dv_sum = dv_part if dv_sum is None else dv_sum + dv_part
            dk_sum = dk_part if dk_sum is None else dk_sum + dk_part
    pair = 2 * HD
    out[:, :pair] = (dq_t[...] * (HD**-0.5)).T.astype(BF)
    out[:, pair : 2 * pair] = (dk_sum * LN2).astype(BF)
    out[:, 2 * pair :] = dv_sum.astype(BF)


def attend_back(probs, qkv, grad_mixed, mixed, inverse, first, pairs, before):
    rows, triple = qkv.shape
    width = triple // 3
    every = width // (2 * HD)

    def column(offset):
        return pl.BlockSpec((rows, 2 * HD), lambda j: (0, offset + j))

    args = (probs, qkv, qkv, qkv, grad_mixed, mixed, inverse)
    specs = [
        pl.BlockSpec((2, rows, rows), lambda j: (first + j, 0, 0)),
        column(first),
        column(every + first),
        column(2 * every + first),
        column(first),
        column(first),
        pl.BlockSpec((1, 2, rows), lambda j: (first + j, 0, 0)),
    ]
    aliases = {}
    if before is not None:
        aliases = {len(args): 0}
        args += (before,)
        specs.append(pl.BlockSpec(memory_space=pl.ANY))
    return call(
        attend_back_body,
        (pairs,),
        (),
        specs,
        pl.BlockSpec((rows, 6 * HD), lambda j: (0, first + j)),
        shape((rows, triple), BF),
        args,
        4 * 2 * rows * rows * 256 * 2 * pairs,
        scratch=[pltpu.VMEM((2 * HD, rows), F32), pltpu.VMEM((rows, rows), BF)],
        aliases=aliases,
    )


def gelu_parts(x):
    below = 0.5 + 0.5 * lax.erf(0.7071067811865476 * x)
    bell = jnp.exp2((-0.5 * LOG2E) * (x * x))
    return x * below, below + (0.3989422804014327 * x) * bell


def middle_body(
    info,
    mixed,
    embedded,
    grad_gelu_low,
    grad_gelu_high,
    cot_act,
    cot_pool,
    w_out,
    gain,
    shift,
    w_up,
    b_up,
    middle,
    normed,
    gelu_out,
    grad_pre,
    grad_attn,
    grad_mixed,
    sums,
    bias_sum,
):
    rows, width = middle.shape
    hidden = w_up.shape[1]
    step = FF_STEP

    @pl.when(pl.program_id(0) == 0)
    def _():
        sums[...] = jnp.zeros_like(sums)
        bias_sum[...] = jnp.zeros_like(bias_sum)

    value = embedded[...].astype(F32) + mm(mixed[...], w_out[...], 1, 0)
    middle[...] = value.astype(BF)
    normal, scale = row_stats(value)
    low = (normal * gain[...] + shift[...]).astype(BF)
    normed[...] = low
    grad_normed = None
    done = None
    coming = mm(low, w_up[:, :step], 1, 0)
    for start in range(0, hidden, step):
        cols = slice(start, start + step)
        pre = coming + b_up[:, cols]
        after = start + step
        if after < hidden:
            coming = mm(low, w_up[:, after : after + step], 1, 0)
        if done is not None:
            grad_normed = done if grad_normed is None else grad_normed + done
        out, slope = gelu_parts(pre)
        gelu_out[:, cols] = out.astype(BF)
        if after <= hidden // 2:
            grad_out = grad_gelu_low[:, cols]
        else:
            grad_out = grad_gelu_high[:, start - hidden // 2 : after - hidden // 2]
        back = (grad_out.astype(F32) * slope).astype(BF)
        grad_pre[:, cols] = back
        bias_sum[:, cols] += jnp.sum(back.astype(F32), axis=0, keepdims=True)
        done = mm(back, w_up[:, cols], 1, 1)
    grad_normed = grad_normed + done
    sums[0:1, :] += jnp.sum(grad_normed * normal, axis=0, keepdims=True)
    sums[1:2, :] += jnp.sum(grad_normed, axis=0, keepdims=True)
    length = info[2]
    live = usable_rows(rows, length)
    pooled = cot_pool[...] / length.astype(F32)
    final = (cot_act[0, 0].astype(F32) + pooled) * live
    total = final + norm_back(grad_normed, normal, scale, gain[...])
    total_low = total.astype(BF)
    grad_attn[...] = total_low
    grad_mixed[...] = mm(total_low, w_out[...], 1, 1).astype(BF)


def middle_rows(
    info, mixed, embedded, low, high, cot_act, cot_pool, w_out, gain, shift, w_up, b_up
):
    rows, width = mixed.shape
    hidden = w_up.shape[1]
    narrow = pl.BlockSpec((ROWS, width), lambda i, s: (i, 0))
    wide = pl.BlockSpec((ROWS, hidden), lambda i, s: (i, 0))
    part = pl.BlockSpec((ROWS, hidden // 2), lambda i, s: (i, 0))
    return call(
        middle_body,
        (rows // ROWS,),
        (info,),
        [
            narrow,
            narrow,
            part,
            part,
            pl.BlockSpec((1, 1, ROWS, width), lambda i, s: (0, 0, i, 0)),
            fixed((1, width)),
            fixed((width, width)),
            fixed((1, width)),
            fixed((1, width)),
            fixed((width, hidden)),
            fixed((1, hidden)),
        ],
        [narrow, narrow, wide, wide, narrow, narrow]
        + [
            pl.BlockSpec((8, width), lambda i, s: (0, 0)),
            pl.BlockSpec((1, hidden), lambda i, s: (0, 0)),
        ],
        [
            shape((rows, width), BF),
            shape((rows, width), BF),
            shape((rows, hidden), BF),
            shape((rows, hidden), BF),
            shape((rows, width), BF),
            shape((rows, width), BF),
            shape((8, width), F32),
            shape((1, hidden), F32),
        ],
        (mixed, embedded, low, high, cot_act, cot_pool, w_out, gain, shift, w_up, b_up),
        2 * rows * width * (2 * width + 2 * hidden),
    )


SAME_QUARTER = (3, 1, 2, 0)


def down_body(height, order, which, left, right_theirs, right_mine, theirs, mine):
    half = right_mine.shape[1]
    both = jnp.concatenate([right_theirs[...], right_mine[...]], axis=1)
    out = mm(left[...], both, 0, 0).astype(BF)
    folds, quarter = theirs.shape[1:3]
    for shard in range(quarter // height):
        for fold in range(folds):
            at = (shard * folds + fold) * height
            rows = slice(shard * height, (shard + 1) * height)
            theirs[0, fold, rows] = out[at : at + height, :half]
            mine[0, fold, rows] = out[at : at + height, half:]


def grad_down_halves(order, which, gelu_out, branch, first, count, height):
    rows, hidden = gelu_out.shape
    width = branch.shape[1]
    half = width // 2
    tall = hidden // 4
    block = (1, hidden // width, width // 4, half)
    return call(
        functools.partial(down_body, height),
        (count,),
        (order, which),
        [
            pl.BlockSpec((rows, tall), lambda j, o, w: (0, o[first + j])),
            pl.BlockSpec((rows, half), lambda j, o, w: (0, 1 - w[0])),
            pl.BlockSpec((rows, half), lambda j, o, w: (0, w[0])),
        ],
        [pl.BlockSpec(block, lambda j, o, w: (j, 0, 0, 0))] * 2,
        [shape((count,) + block[1:], BF)] * 2,
        (gelu_out, branch, branch),
        rows * hidden * half * count,
    )


def place_quarters(places, value, theirs, mine, rows=None):
    quarter = value.shape[0] // 4
    lanes = mine.shape[3]
    for i in range(4):
        block = value[i * quarter : (i + 1) * quarter].astype(BF)
        theirs[places[4 + i], 0, :quarter] = block[:, :lanes]
        mine[places[i], 0, :quarter] = block[:, lanes:]


def up_body(
    places, which, normed, pre_theirs, pre_mine, mixed, attn_theirs, attn_mine, theirs, mine
):
    step = pl.program_id(0)
    last = pl.num_programs(0) - 1

    @pl.when(step < last)
    def _():
        both = jnp.concatenate([pre_theirs[...], pre_mine[...]], axis=1)
        place_quarters(places, mm(normed[...], both, 0, 0), theirs, mine)

    @pl.when(step == last)
    def _():
        both = jnp.concatenate([attn_theirs[...], attn_mine[...]], axis=1)
        place_quarters(places, mm(mixed[...], both, 0, 0), theirs, mine)


def column_call(body, order, which, grid, lanes, quarter, specs, args, flops, vmem=40):
    return call(
        body,
        (grid,),
        (order, which),
        specs,
        [pl.BlockSpec((4, 1, quarter, lanes), lambda j, o, w: (0, j, 0, 0))] * 2,
        [shape((4, grid, quarter, lanes), BF)] * 2,
        args,
        flops,
        vmem=vmem,
    )


def grad_up_halves(order, which, normed, grad_pre, mixed, grad_attn):
    rows, width = normed.shape
    half = width // 2
    lanes = half
    steps = grad_pre.shape[1] // 2 // lanes

    def hidden_block(core):
        return pl.BlockSpec(
            (rows, lanes), lambda j, o, w: (0, core(w) * steps + jnp.minimum(j, steps - 1))
        )

    specs = [
        fixed((rows, width)),
        hidden_block(lambda w: 1 - w[0]),
        hidden_block(lambda w: w[0]),
        fixed((rows, width)),
        pl.BlockSpec((rows, half), lambda j, o, w: (0, 1 - w[0])),
        pl.BlockSpec((rows, half), lambda j, o, w: (0, w[0])),
    ]
    return column_call(
        up_body,
        order,
        which,
        steps + 1,
        lanes,
        width // 4,
        specs,
        (normed, grad_pre, grad_pre, mixed, grad_attn, grad_attn),
        4 * rows * width * (steps * lanes + half),
    )


def qkv_body(places, which, normed, grad_theirs, grad_mine, theirs, mine):
    both = jnp.concatenate([grad_theirs[...], grad_mine[...]], axis=1)
    place_quarters(places, mm(normed[...], both, 0, 0), theirs, mine)


def grad_qkv_halves(order, which, normed, grad_qkv):
    rows, width = normed.shape
    steps = 3
    lanes = grad_qkv.shape[1] // 2 // steps
    specs = [
        fixed((rows, width)),
        pl.BlockSpec((rows, lanes), lambda j, o, w: (0, (1 - w[0]) * steps + j)),
        pl.BlockSpec((rows, lanes), lambda j, o, w: (0, w[0] * steps + j)),
    ]
    return column_call(
        qkv_body,
        order,
        which,
        steps,
        lanes,
        width // 4,
        specs,
        (normed, grad_qkv, grad_qkv),
        4 * rows * width * steps * lanes,
    )


def kernel_body(
    places, which, pixels, grad_theirs, grad_mine, sums_one, sums_two, bias, theirs, mine
):
    both = jnp.concatenate([grad_theirs[...], grad_mine[...]], axis=1)
    out = mm(pixels[0, 0], both, 0, 0)
    place_quarters(places, out, theirs, mine)
    quarter = out.shape[0] // 4
    lanes = mine.shape[3]
    width = sums_one.shape[1] // 4
    folds = bias.shape[1] // 4 // width
    for i in range(4):
        cols = slice(i * width, (i + 1) * width)
        rows = [sums_one[0:1, cols], sums_one[1:2, cols], sums_two[0:1, cols], sums_two[1:2, cols]]
        for n in range(folds):
            at = (i * folds + n) * width
            rows.append(bias[:, at : at + width])
        rows.append(jnp.zeros((16 - len(rows), width), F32))
        block = jnp.concatenate(
            [jnp.concatenate(rows, axis=0), jnp.zeros((16, lanes - width), F32)], axis=1
        ).astype(BF)
        theirs[places[4 + i], 0, quarter:] = block
        mine[places[i], 0, quarter:] = block


def grad_kernel_halves(order, which, pixels, grad, sums_one, sums_two, bias):
    rows, patch = pixels.shape[2:]
    half = grad.shape[1] // 2
    specs = [
        pl.BlockSpec((1, 1, rows, patch), lambda j, o, w: (0, w[1], 0, 0)),
        pl.BlockSpec((rows, half), lambda j, o, w: (0, 1 - w[0])),
        pl.BlockSpec((rows, half), lambda j, o, w: (0, w[0])),
        fixed(sums_one.shape),
        fixed(sums_two.shape),
        fixed(bias.shape),
    ]
    return column_call(
        kernel_body,
        order,
        which,
        1,
        half,
        patch // 4 + 16,
        specs,
        (pixels, grad, grad, sums_one, sums_two, bias),
        4 * rows * patch * half,
        vmem=60,
    )


def first_back_body(grad_qkv, w_qkv, embedded, gain, grad_middle, out, sums):
    width = out.shape[1]
    pair = 2 * HD

    @pl.when(pl.program_id(0) == 0)
    def _():
        sums[...] = jnp.zeros_like(sums)

    grad = None
    for i in range(3):
        starts = range(i * pair, 3 * width, 3 * pair)
        value = jnp.concatenate([grad_qkv[:, at : at + pair] for at in starts], axis=1)
        part = mm(value, w_qkv[:, i * width : (i + 1) * width], 1, 1)
        grad = part if grad is None else grad + part
    normal, scale = row_stats(embedded[...].astype(F32))
    sums[0:1, :] += jnp.sum(grad * normal, axis=0, keepdims=True)
    sums[1:2, :] += jnp.sum(grad, axis=0, keepdims=True)
    out[...] = (grad_middle[...].astype(F32) + norm_back(grad, normal, scale, gain[...])).astype(BF)


def first_back(grad_qkv, w_qkv, embedded, gain, grad_middle):
    rows, width = embedded.shape
    narrow = pl.BlockSpec((ROWS, width), lambda i: (i, 0))
    return call(
        first_back_body,
        (rows // ROWS,),
        (),
        [
            pl.BlockSpec((ROWS, 3 * width), lambda i: (i, 0)),
            fixed(w_qkv.shape),
            narrow,
            fixed((1, width)),
            narrow,
        ],
        [narrow, pl.BlockSpec((8, width), lambda i: (0, 0))],
        [shape((rows, width), BF), shape((8, width), F32)],
        (grad_qkv, w_qkv, embedded, gain, grad_middle),
        2 * rows * width * 3 * width,
    )


def last_body(info, middle, gelu_out, w_down, activations, pooled):
    rows = middle.shape[0]
    length = info[2]

    @pl.when(pl.program_id(0) == 0)
    def _():
        pooled[...] = jnp.zeros_like(pooled)

    final = middle[...].astype(F32) + mm(gelu_out[...], w_down[...], 1, 0)
    final = final * usable_rows(rows, length)
    activations[0, 0] = final.astype(BF)
    pooled[0] += jnp.sum(final, axis=0, keepdims=True)

    @pl.when(pl.program_id(0) == pl.num_programs(0) - 1)
    def _():
        pooled[...] = pooled[...] / length.astype(F32)


def last_rows(info, middle, gelu_out, w_down):
    rows, width = middle.shape
    hidden = w_down.shape[0]
    return call(
        last_body,
        (rows // ROWS,),
        (info,),
        [
            pl.BlockSpec((ROWS, width), lambda i, s: (i, 0)),
            pl.BlockSpec((ROWS, hidden), lambda i, s: (i, 0)),
            fixed((hidden, width)),
        ],
        [
            pl.BlockSpec((1, 1, ROWS, width), lambda i, s: (0, 0, i, 0)),
            pl.BlockSpec((1, 1, width), lambda i, s: (0, 0, 0)),
        ],
        [shape((1, 1, rows, width), BF), shape((1, 1, width), F32)],
        (middle, gelu_out, w_down),
        2 * rows * width * hidden,
    )


def pixel_body(grad_embedded, kernel, pixel_grad):
    pixel_grad[0, 0] = mm(grad_embedded[...], kernel[...], 1, 1)


def pixel_rows(grad_embedded, kernel):
    rows, width = grad_embedded.shape
    patch = kernel.shape[0]
    return call(
        pixel_body,
        (rows // ROWS,),
        (),
        [pl.BlockSpec((ROWS, width), lambda i: (i, 0)), fixed((patch, width))],
        pl.BlockSpec((1, 1, ROWS, patch), lambda i: (0, 0, i, 0)),
        shape((1, 1, rows, patch), F32),
        (grad_embedded, kernel),
        2 * rows * width * patch,
    )


def base_body(order, order_far, which, resize, near, far, out, work):
    half = near.shape[2]
    quarter = near.shape[1]
    patch = resize.shape[1]
    for j in range(4):
        rows = pl.ds(pl.multiple_of(order[j] * quarter, quarter), quarter)
        work[which[0], rows, :] = near[j]
        rows = pl.ds(pl.multiple_of(order_far[j] * quarter, quarter), quarter)
        work[1 - which[0], rows, :] = far[j]
    for c in range(out.shape[0]):
        for h in range(2):
            out[c, :, h * half : (h + 1) * half] = mm(
                resize[...], work[h, c * patch : (c + 1) * patch, :], 1, 0
            )


def base_grad_of(order, order_far, which, resize, near, far, channels):
    pixels, patch = resize.shape
    _, quarter, half = near.shape
    return call(
        base_body,
        (1,),
        (order, order_far, which),
        [fixed(resize.shape), fixed(near.shape), fixed(far.shape)],
        fixed((channels, pixels, 2 * half)),
        shape((channels, pixels, 2 * half), F32),
        (resize, near, far),
        2 * channels * pixels * patch * 2 * half,
        scratch=[pltpu.VMEM((2, 4 * quarter, half), BF)],
    )


class Links:
    def __init__(self):
        self.parts = lax.axis_size("pix")
        self.count = lax.axis_size("tok")
        self.pix = lax.axis_index("pix")
        self.tok = lax.axis_index("tok")
        self.core = self.tok % 2
        self.chips = self.count // 2
        self.near = 1 + self.core
        self.far = 2 - self.core

    def swap(self, value, partner):
        pairs = []
        for p in range(self.parts):
            for t in range(self.count):
                q, u = partner(p, t)
                pairs.append((p * self.count + t, q * self.count + u))
        return lax.ppermute(value, ("pix", "tok"), pairs)

    def core_swap(self, value):
        return self.swap(value, lambda p, t: (p, t ^ 1))

    def first_swap(self, value):
        return self.swap(value, lambda p, t: (p ^ (1 + t % 2), t))

    def second_swap(self, value):
        return self.swap(value, lambda p, t: (p ^ (2 - t % 2), t))

    def chip_swap(self, value, bit):
        return self.swap(value, lambda p, t: (p, t ^ (2 << bit)))

    def quarters(self, near, far):
        pix = self.pix
        return jnp.stack([pix ^ near, pix ^ 3, pix, pix ^ far]).astype(jnp.int32)


def places_of(order):
    return jnp.argmax(order[None, :] == jnp.arange(4)[:, None], axis=1).astype(jnp.int32)


def together(*values):
    return lax.optimization_barrier(values)


def add(a, b, dtype=BF):
    return (a.astype(F32) + b.astype(F32)).astype(dtype)


def combine(arrived, mine):
    return add(arrived[:2], mine[:2]), add(arrived[2:], mine[2:])


class Order:
    def __init__(self):
        self.last = ()

    def __call__(self, work, *values, keep=False):
        flat, tree = jax.tree.flatten(values)
        count = len(flat)
        if self.last:
            flat = list(together(*flat, *self.last))[:count]
        result = work(*jax.tree.unflatten(tree, flat))
        if not keep:
            self.last = tuple(jax.tree.leaves(result))
        return result


class Chain:
    def __init__(self, order, links, away, keep):
        self.order, self.links = order, links
        self.stage = 0
        self.last = 1 + links.chips.bit_length() - 1
        self.arrived = links.first_swap(away)
        self.staying = keep

    def advance(self):
        links, stage = self.links, self.stage
        if stage > self.last:
            return

        def quarters(arrived, staying):
            return add(arrived[1], staying[1]), add(arrived[0], staying[0])

        def split(value, bit):
            own = (links.tok >> (bit + 1)) & 1
            blocks, left, height, lanes = value.shape
            value = value.reshape(blocks, left // 2, 2, height, lanes)
            leaving = lax.dynamic_index_in_dim(value, 1 - own, 2, keepdims=False)
            return leaving, lax.dynamic_index_in_dim(value, own, 2, keepdims=False)

        def pix_sum(arrived, staying):
            value = add(arrived, staying)
            blocks, rows, lanes = value.shape
            return split(value.reshape(blocks, links.chips, rows // links.chips, lanes), 0)

        def chip_sum(arrived, staying):
            return split(add(arrived, staying), stage - 1)

        def last_sum(arrived, staying):
            return add(arrived, staying, F32)[:, 0]

        work = quarters if stage == 0 else pix_sum if stage == 1 else chip_sum
        if stage == self.last:
            self.value = self.order(last_sum, self.arrived, self.staying, keep=True)
        else:
            leaving, self.staying = self.order(work, self.arrived, self.staying)
            if stage == 0:
                self.arrived = links.second_swap(leaving)
            else:
                self.arrived = links.chip_swap(leaving, stage - 1)
        self.stage += 1

    def finish(self):
        while self.stage <= self.last:
            self.advance()
        return self.value


def own_rows(links, value):
    blocks, rows, lanes = value.shape
    pair = value.reshape(blocks, 2, rows // 2, lanes)
    mine = lax.dynamic_index_in_dim(pair, links.core, 1, keepdims=False)
    arrived = links.core_swap(
        lax.dynamic_index_in_dim(pair, 1 - links.core, 1, keepdims=False)
    )
    first = links.core == 0
    return jnp.where(first, mine, arrived), jnp.where(first, arrived, mine)


def local(
    pixels,
    lengths,
    base_kernel,
    resize,
    gain_one,
    shift_one,
    w_qkv,
    w_out,
    gain_two,
    shift_two,
    w_up,
    b_up,
    w_down,
    cot_act,
    cot_pool,
):
    links = Links()
    turn = Order()
    seq_len = pixels.shape[2]
    width = w_qkv.shape[0]
    hidden = w_up.shape[1]
    channels = base_kernel.shape[0]
    half = width // 2
    core = links.core
    own_length = lax.dynamic_index_in_dim(lengths[0], links.pix, 0, keepdims=False)
    info = jnp.stack([links.pix, core, own_length]).astype(jnp.int32)
    mine = jnp.stack([core, links.pix]).astype(jnp.int32)
    order = links.quarters(links.near, links.far)
    order_theirs = links.quarters(links.far, links.near)
    places = jnp.concatenate([places_of(order), places_of(order_theirs)])
    gain_one, shift_one = gain_one[None], shift_one[None]
    gain_two, shift_two, b_up = gain_two[None], shift_two[None], b_up[None]
    cot_pool = cot_pool[0]

    piece = partial_kernel(resize, base_kernel)
    piece = add(links.first_swap(piece), piece)
    branch, gelu_low = cot_branch(info, cot_act, cot_pool, w_down, 0)
    piece, branch, gelu_low = together(piece, branch, gelu_low)
    piece = add(links.second_swap(piece), piece)
    (gelu_high,) = cot_branch(info, cot_act, cot_pool, w_down, 1)
    piece, gelu_high = together(piece, gelu_high)
    other = links.core_swap(piece)
    kernel = jnp.concatenate(
        [jnp.where(core == 0, piece, other), jnp.where(core == 0, other, piece)], axis=1
    )

    lane = jnp.arange(2 * HD)[None, None, :]
    slot = jnp.array([HD, 0])[:, None, None]
    blocked = (jnp.arange(seq_len) >= own_length)[None, :, None] & (lane == slot)
    extra = jnp.where(blocked, -1e30, 0.0).astype(BF)

    embedded, normed, qkv = embed_rows(info, pixels, kernel, gain_one, shift_one, w_qkv)
    probs, mixed, inverse = attend(qkv, extra)
    (
        middle,
        normed_two,
        gelu_out,
        grad_pre,
        grad_attn,
        grad_mixed,
        sums_two,
        bias_sum,
    ) = middle_rows(
        info,
        mixed,
        embedded,
        gelu_low,
        gelu_high,
        cot_act,
        cot_pool,
        w_out,
        gain_two,
        shift_two,
        w_up,
        b_up,
    )

    shard = width // (links.parts * links.chips)
    up_theirs, up_mine = turn(
        lambda *a: grad_up_halves(places, mine, *a), normed_two, grad_pre, mixed, grad_attn
    )
    up_arrived = links.core_swap(up_theirs)
    away_theirs, away_mine = turn(
        lambda *a: grad_down_halves(order, mine, *a, 0, 2, shard), gelu_out, branch
    )
    away_arrived = links.core_swap(away_theirs)
    up_arrived, gelu_last = together(up_arrived, gelu_out)
    keep_theirs, keep_mine = turn(
        lambda *a: grad_down_halves(order, mine, *a, 2, 2, shard), gelu_last, branch
    )
    keep_arrived = links.core_swap(keep_theirs)
    def combine_wide(up_arrived, up_mine, away_arrived, away_mine, keep_arrived, keep_mine):
        up_away, up_keep = combine(up_arrived, up_mine)
        away = add(jnp.stack([keep_arrived[1], away_arrived[1]]), away_mine)
        keep = add(jnp.stack([keep_arrived[0], away_arrived[0]]), keep_mine)
        return (
            jnp.concatenate([up_away, away], axis=1),
            jnp.concatenate([up_keep, keep], axis=1),
        )

    wide = Chain(
        turn,
        links,
        *turn(
            combine_wide, up_arrived, up_mine, away_arrived, away_mine, keep_arrived, keep_mine
        ),
    )

    every = width // (2 * HD)
    cuts = [every // 3 * n for n in range(3)] + [every]

    def back(n, before):
        return turn(
            lambda probs, *a: attend_back(
                probs, qkv, grad_mixed, mixed, inverse, cuts[n], cuts[n + 1] - cuts[n], *a
            ),
            probs,
            before,
        )

    grad_qkv = back(0, None)
    grad_qkv = back(1, grad_qkv)
    grad_qkv = back(2, grad_qkv)
    wide.advance()

    three_theirs, three_mine = turn(
        lambda *a: grad_qkv_halves(places, mine, *a), normed, grad_qkv
    )
    three_arrived = links.core_swap(three_theirs)

    grad_embedded, sums_one = turn(
        lambda *a: first_back(*a, w_qkv, embedded, gain_one, grad_attn), grad_qkv
    )
    three_away, three_keep = turn(combine, three_arrived, three_mine)
    three = Chain(turn, links, three_away, three_keep)
    kernel_theirs, kernel_mine = turn(
        lambda *a: grad_kernel_halves(places, mine, pixels, *a, sums_two, bias_sum),
        grad_embedded,
        sums_one,
    )
    arrived = links.core_swap(kernel_theirs)
    wide.advance()
    away, keep = turn(combine, arrived, kernel_mine)
    arrived = links.first_swap(away)
    leaving, staying = turn(
        lambda a, b: (add(a[1], b[1]), add(a[0], b[0])), arrived, keep
    )
    arrived = links.second_swap(leaving)
    three.advance()
    quarter = turn(add, arrived, staying)
    arrived = links.chip_swap(quarter, 0)
    pixel_grad = turn(pixel_rows, grad_embedded, kernel)
    wide.advance()
    quarter = turn(add, arrived, quarter)
    arrived = links.chip_swap(quarter, 1)
    three.advance()
    activations, pooled = turn(
        lambda *a: last_rows(info, *a), middle, gelu_out, w_down
    )
    quarter = turn(add, arrived, quarter)
    for bit in range(2, links.chips.bit_length() - 1):
        arrived = links.chip_swap(quarter, bit)
        quarter = turn(add, arrived, quarter)
    vectors = quarter[0, -16:, : width // links.parts].astype(F32)
    quarter = quarter[0, :-16]
    arrived = links.second_swap(quarter)
    wide.advance()
    three.advance()
    pair = turn(lambda a, b: jnp.stack([a, b]), quarter, arrived)
    arrived = links.first_swap(pair)
    full = turn(lambda a, b: jnp.concatenate([a, b], axis=0), arrived, pair)
    arrived = links.core_swap(full)
    base_grad = turn(
        lambda *a: base_grad_of(order, order_theirs, mine, resize, *a, channels), full, arrived
    )
    wide, three = wide.finish(), three.finish()

    height = width // (links.parts * links.count)
    tall = hidden // (links.parts * links.count)
    folds = hidden // width
    wide_low, wide_high = own_rows(links, wide[: folds + 1])
    grad_up = jnp.concatenate([*wide_low[:folds], *wide_high[:folds]], axis=1)
    grad_out = jnp.concatenate([wide_low[folds], wide_high[folds]], axis=1)
    part = wide[folds + 1 :].reshape(2, -1, half)
    down_mine = lax.dynamic_index_in_dim(part, core, 0, keepdims=False)
    down_arrived = links.core_swap(
        lax.dynamic_index_in_dim(part, 1 - core, 0, keepdims=False)
    )
    down = jnp.concatenate(
        [
            jnp.where(core == 0, down_mine, down_arrived),
            jnp.where(core == 0, down_arrived, down_mine),
        ],
        axis=1,
    )
    three_low, three_high = own_rows(links, three)
    three_low = jnp.concatenate(list(three_low), axis=1)
    three_high = jnp.concatenate(list(three_high), axis=1)
    pair = 2 * HD
    pieces = []
    for i in range(3):
        for value in (three_low, three_high):
            for at in range(i * pair, value.shape[1], 3 * pair):
                pieces.append(value[:, at : at + pair])
    grad_qkv = jnp.concatenate(pieces, axis=1)
    small = lax.dynamic_slice_in_dim(vectors[:4], links.tok * height, height, 1)
    grad_bias = lax.dynamic_slice_in_dim(
        vectors[4 : 4 + folds].reshape(-1), links.tok * tall, tall, 0
    )
    return (
        activations,
        pooled,
        pixel_grad,
        base_grad,
        small[0],
        small[1],
        grad_qkv,
        grad_out,
        small[2],
        small[3],
        grad_up,
        grad_bias,
        down,
    )


def solution(mesh):
    placed = (
        P("tok", None, None, None),
        P("tok", None),
        P(None, "pix", None),
        P("pix", None),
        P(),
        P(),
        P(),
        P(),
        P(),
        P(),
        P(),
        P(),
        P(),
        P("tok", "pix", None, None),
        P("tok", "pix", None),
    )
    return jax.shard_map(
        local,
        mesh=mesh,
        in_specs=placed,
        out_specs=(
            P("tok", "pix", None, None),
            P("tok", "pix", None),
            P("tok", "pix", None, None),
            P(None, "pix", None),
            P(("pix", "tok")),
            P(("pix", "tok")),
            P(("pix", "tok"), None),
            P(("pix", "tok"), None),
            P(("pix", "tok")),
            P(("pix", "tok")),
            P(("pix", "tok"), None),
            P(("pix", "tok")),
            P(("pix", "tok"), None),
        ),
        check_vma=False,
    )
```

```python
import functools

import jax
import jax.numpy as jnp
from jax import lax
from jax.experimental import pallas as pl
from jax.experimental.pallas import tpu as pltpu
from jax.sharding import PartitionSpec as P

HD = 64
EPSILON = 1e-06
LOG2E = 1.4426950408889634
LN2 = 0.6931471805599453
ROWS = 256
CHUNK = 512
FF_STEP = 256
MIB = 1 << 20
BF = jnp.bfloat16
F32 = jnp.float32


def mm(lhs, rhs, lhs_dim, rhs_dim):
    return lax.dot_general(
        lhs, rhs, (((lhs_dim,), (rhs_dim,)), ((), ())), preferred_element_type=F32
    )


def call(body, grid, prefetch, in_specs, out_specs, out_shape, args, flops, scratch=(), vmem=40, aliases=None, light=False):
    moved = sum(a.size * a.dtype.itemsize for a in args)
    moved += sum(o.size * o.dtype.itemsize for o in jax.tree.leaves(out_shape))
    return pl.pallas_call(
        body,
        grid_spec=pltpu.PrefetchScalarGridSpec(
            num_scalar_prefetch=len(prefetch),
            grid=grid,
            in_specs=in_specs,
            out_specs=out_specs,
            scratch_shapes=list(scratch),
        ),
        out_shape=out_shape,
        compiler_params=pltpu.CompilerParams(
            dimension_semantics=("arbitrary",) * len(grid), vmem_limit_bytes=vmem * MIB
        ),
        input_output_aliases=aliases or {},
        cost_estimate=pl.CostEstimate(
            flops=1 if light else int(flops),
            bytes_accessed=1 if light else int(moved),
            transcendentals=0,
        ),
    )(*prefetch, *args)


def shape(dims, dtype):
    return jax.ShapeDtypeStruct(dims, dtype)


def fixed(dims):
    zeros = (0,) * len(dims)
    return pl.BlockSpec(dims, lambda *a: zeros, pipeline_mode=pl.Buffered(1))


def row_stats(x):
    mean = jnp.mean(x, axis=-1, keepdims=True)
    centered = x - mean
    var = jnp.mean(centered * centered, axis=-1, keepdims=True)
    scale = lax.rsqrt(var + EPSILON)
    return centered * scale, scale


def norm_back(grad, normal, scale, gain):
    e = grad * gain
    mean_e = jnp.mean(e, axis=-1, keepdims=True)
    mean_en = jnp.mean(e * normal, axis=-1, keepdims=True)
    return scale * (e - mean_e - normal * mean_en)


def usable_rows(rows, length):
    start = pl.program_id(0) * rows
    index = lax.broadcasted_iota(jnp.int32, (rows, 1), 0) + start
    return (index < length).astype(F32)


def partial_body(resize, base, out):
    half = out.shape[1]
    start = pl.multiple_of(lax.axis_index("tok") % 2 * half, half)
    out[...] = mm(resize[...], base[0, :, pl.ds(start, half)], 0, 0).astype(BF)


def partial_kernel(resize, base):
    channels, pixels, width = base.shape
    patch = resize.shape[1]
    half = width // 2
    return call(
        partial_body,
        (channels,),
        (),
        [fixed((pixels, patch)), pl.BlockSpec((1, pixels, width), lambda c: (c, 0, 0))],
        pl.BlockSpec((patch, half), lambda c: (c, 0)),
        shape((channels * patch, half), BF),
        (resize, base),
        2 * channels * pixels * patch * half,
    )


def cot_body(info, cot_act, cot_pool, w_down, *outs):
    length = info[2]
    live = usable_rows(cot_act.shape[2], length)
    pooled = cot_pool[...] / length.astype(F32)
    value = ((cot_act[0, 0].astype(F32) + pooled) * live).astype(BF)
    if len(outs) > 1:
        outs[0][...] = value
    outs[-1][...] = mm(value, w_down[...], 1, 1).astype(BF)


def cot_branch(info, cot_act, cot_pool, w_down, part):
    rows, width = cot_act.shape[2:]
    hidden = w_down.shape[0] // 2
    narrow = pl.BlockSpec((ROWS, width), lambda i, s: (i, 0))
    wide = pl.BlockSpec((ROWS, hidden), lambda i, s: (i, 0))
    lead = part == 0
    return call(
        cot_body,
        (rows // ROWS,),
        (info,),
        [
            pl.BlockSpec((1, 1, ROWS, width), lambda i, s: (0, 0, i, 0)),
            fixed((1, width)),
            pl.BlockSpec((hidden, width), lambda i, s: (part, 0), pipeline_mode=pl.Buffered(1)),
        ],
        [narrow, wide] if lead else [wide],
        ([shape((rows, width), BF)] if lead else []) + [shape((rows, hidden), BF)],
        (cot_act, cot_pool, w_down),
        2 * rows * width * hidden,
    )


def embed_body(info, pixels, kernel, gain, shift, w_qkv, embedded, normed, qkv):
    width = embedded.shape[1]
    value = mm(pixels[0, 0], kernel[...], 1, 0).astype(BF)
    embedded[...] = value
    normal, _ = row_stats(value.astype(F32))
    low = (normal * gain[...] + shift[...]).astype(BF)
    normed[...] = low
    for part in range(3):
        cols = slice(part * width, (part + 1) * width)
        product = mm(low, w_qkv[:, cols], 1, 0)
        if part == 0:
            product = product * (HD**-0.5 * LOG2E)
        qkv[:, cols] = product.astype(BF)


def embed_rows(info, pixels, kernel, gain, shift, w_qkv):
    rows, patch = pixels.shape[2:]
    width, triple = w_qkv.shape
    return call(
        embed_body,
        (rows // ROWS,),
        (info,),
        [
            pl.BlockSpec((1, 1, ROWS, patch), lambda i, s: (0, s[0], i, 0)),
            fixed((patch, width)),
            fixed((1, width)),
            fixed((1, width)),
            fixed((width, triple)),
        ],
        [
            pl.BlockSpec((ROWS, width), lambda i, s: (i, 0)),
            pl.BlockSpec((ROWS, width), lambda i, s: (i, 0)),
            pl.BlockSpec((ROWS, triple), lambda i, s: (i, 0)),
        ],
        [shape((rows, width), BF), shape((rows, width), BF), shape((rows, triple), BF)],
        (pixels, kernel, gain, shift, w_qkv),
        2 * rows * width * (patch + triple),
    )


def attend_heads(exact, q_t, k, v_t, extra, probs, inverse, mixed_t):
    rows = k.shape[0]
    lane = lax.broadcasted_iota(jnp.int32, (1, 2 * HD), 1)
    first_row = lax.broadcasted_iota(jnp.int32, (HD, rows), 0) == 0
    ones = jnp.where(first_row, 1.0, 0.0).astype(BF)
    sides = []
    for head in range(2):
        own = slice(head * HD, (head + 1) * HD)
        chosen = jnp.where((lane >= HD) == (head == 1), 1.0, 0.0).astype(BF)
        stack = [q_t[own], ones] if head == 0 else [ones, q_t[own]]
        sides.append((k[...] * chosen + extra[head], jnp.concatenate(stack, axis=0)))
    steps = [(head, start) for head in range(2) for start in range(0, rows, CHUNK)]

    def score(step):
        head, start = step
        return mm(sides[head][0], sides[head][1][:, start : start + CHUNK], 1, 0)

    coming = score(steps[0])
    for n, (head, start) in enumerate(steps):
        own = slice(head * HD, (head + 1) * HD)
        cols = slice(start, start + CHUNK)
        scores = coming
        if n + 1 < len(steps):
            coming = score(steps[n + 1])
        if exact:
            scores = scores - jnp.max(scores, axis=0, keepdims=True)
        power = jnp.exp2(scores)
        total = 1.0 / jnp.sum(power, axis=0, keepdims=True)
        low = power.astype(BF)
        probs[head, :, cols] = low
        inverse[0, head : head + 1, cols] = total
        mixed_t[own, cols] = mm(v_t[own], low, 1, 0) * total


def attend_body(q, k, v, extra, probs, mixed, inverse, mixed_t):
    q_t = q[...].T
    v_t = v[...].T

    def longest(x_t, head):
        square = jnp.square(x_t[head * HD : (head + 1) * HD].astype(F32))
        return jnp.max(jnp.sum(square, axis=0, keepdims=True))

    k_t = k[...].T
    plain = jnp.logical_and(
        longest(q_t, 0) * longest(k_t, 0) <= 3600.0, longest(q_t, 1) * longest(k_t, 1) <= 3600.0
    )
    args = (q_t, k, v_t, extra, probs, inverse, mixed_t)

    @pl.when(plain)
    def _():
        attend_heads(False, *args)

    @pl.when(jnp.logical_not(plain))
    def _():
        attend_heads(True, *args)

    mixed[...] = mixed_t[...].T.astype(BF)


def attend(qkv, extra):
    rows, triple = qkv.shape
    width = triple // 3
    pairs = width // (2 * HD)
    return call(
        attend_body,
        (pairs,),
        (),
        [
            pl.BlockSpec((rows, 2 * HD), lambda j: (0, j)),
            pl.BlockSpec((rows, 2 * HD), lambda j: (0, pairs + j)),
            pl.BlockSpec((rows, 2 * HD), lambda j: (0, 2 * pairs + j)),
            fixed((2, rows, 2 * HD)),
        ],
        [
            pl.BlockSpec((2, rows, rows), lambda j: (j, 0, 0)),
            pl.BlockSpec((rows, 2 * HD), lambda j: (0, j)),
            pl.BlockSpec((1, 2, rows), lambda j: (j, 0, 0)),
        ],
        [
            shape((2 * pairs, rows, rows), BF),
            shape((rows, width), BF),
            shape((pairs, 2, rows), F32),
        ],
        (qkv, qkv, qkv, extra),
        2 * 2 * rows * rows * 256 * 2 * pairs,
        scratch=[pltpu.VMEM((2 * HD, rows), F32)],
    )


def attend_back_body(probs, q, k, v, grad, mixed, inverse, *refs):
    out, dq_t, score_grad = refs[-3:]
    rows = q.shape[0]
    lane = lax.broadcasted_iota(jnp.int32, (1, 2 * HD), 1)
    index = lax.broadcasted_iota(jnp.int32, (HD, rows), 0)
    grad_t = grad[...].T.astype(F32)
    mixed_t = mixed[...].T.astype(F32)
    k_t = k[...].T
    scaled = []
    sides = []
    for head in range(2):
        own = slice(head * HD, (head + 1) * HD)
        total = inverse[0, head : head + 1, :]
        scaled.append((grad_t[own] * total).astype(BF))
        inner = -jnp.sum(grad_t[own] * mixed_t[own], axis=0, keepdims=True) * total
        high = inner.astype(BF).astype(F32)
        sides.append(
            jnp.where(index == 0, high, jnp.where(index == 1, inner - high, 0.0)).astype(BF)
        )
    grad_low = jnp.concatenate(scaled, axis=0).T
    dk_sum = None
    dv_sum = None
    own_lanes = []
    factors = []
    for head in range(2):
        other = (1 - head) * HD
        chosen = jnp.where((lane >= HD) == (head == 1), 1.0, 0.0).astype(BF)
        units = jnp.where((lane == other) | (lane == other + 1), 1.0, 0.0).astype(BF)
        stack = [scaled[0], sides[0]] if head == 0 else [sides[1], scaled[1]]
        own_lanes.append(chosen)
        factors.append((v[...] * chosen + units, jnp.concatenate(stack, axis=0)))
    steps = [(head, start) for head in range(2) for start in range(0, rows, CHUNK)]

    def prob_grad(step):
        head, start = step
        return mm(factors[head][0], factors[head][1][:, start : start + CHUNK], 1, 0)

    coming = prob_grad(steps[0])
    for n, (head, start) in enumerate(steps):
        own = slice(head * HD, (head + 1) * HD)
        cols = slice(start, start + CHUNK)
        shifted = coming
        if n + 1 < len(steps):
            coming = prob_grad(steps[n + 1])
        low = (probs[head, :, cols].astype(F32) * shifted).astype(BF)
        score_grad[:, cols] = low
        dq_t[own, cols] = mm(k_t[own], low, 1, 0)
        if start + CHUNK == rows:
            dv_part = mm(probs[head], grad_low * own_lanes[head], 1, 0)
            dk_part = mm(score_grad[...], q[...] * own_lanes[head], 1, 0)
            dv_sum = dv_part if dv_sum is None else dv_sum + dv_part
            dk_sum = dk_part if dk_sum is None else dk_sum + dk_part
    pair = 2 * HD
    out[:, :pair] = (dq_t[...] * (HD**-0.5)).T.astype(BF)
    out[:, pair : 2 * pair] = (dk_sum * LN2).astype(BF)
    out[:, 2 * pair :] = dv_sum.astype(BF)


def attend_back(probs, qkv, grad_mixed, mixed, inverse, first, pairs, before):
    rows, triple = qkv.shape
    width = triple // 3
    every = width // (2 * HD)

    def column(offset):
        return pl.BlockSpec((rows, 2 * HD), lambda j: (0, offset + j))

    args = (probs, qkv, qkv, qkv, grad_mixed, mixed, inverse)
    specs = [
        pl.BlockSpec((2, rows, rows), lambda j: (first + j, 0, 0)),
        column(first),
        column(every + first),
        column(2 * every + first),
        column(first),
        column(first),
        pl.BlockSpec((1, 2, rows), lambda j: (first + j, 0, 0)),
    ]
    aliases = {}
    if before is not None:
        aliases = {len(args): 0}
        args += (before,)
        specs.append(pl.BlockSpec(memory_space=pl.ANY))
    return call(
        attend_back_body,
        (pairs,),
        (),
        specs,
        pl.BlockSpec((rows, 6 * HD), lambda j: (0, first + j)),
        shape((rows, triple), BF),
        args,
        4 * 2 * rows * rows * 256 * 2 * pairs,
        scratch=[pltpu.VMEM((2 * HD, rows), F32), pltpu.VMEM((rows, rows), BF)],
        aliases=aliases,
    )


def gelu_parts(x):
    below = 0.5 + 0.5 * lax.erf(0.7071067811865476 * x)
    bell = jnp.exp2((-0.5 * LOG2E) * (x * x))
    return x * below, below + (0.3989422804014327 * x) * bell


def middle_body(
    info,
    mixed,
    embedded,
    grad_gelu_low,
    grad_gelu_high,
    cot_act,
    cot_pool,
    w_out,
    gain,
    shift,
    w_up,
    b_up,
    middle,
    normed,
    gelu_out,
    grad_pre,
    grad_attn,
    grad_mixed,
    sums,
    bias_sum,
):
    rows, width = middle.shape
    hidden = w_up.shape[1]
    step = FF_STEP

    @pl.when(pl.program_id(0) == 0)
    def _():
        sums[...] = jnp.zeros_like(sums)
        bias_sum[...] = jnp.zeros_like(bias_sum)

    value = embedded[...].astype(F32) + mm(mixed[...], w_out[...], 1, 0)
    middle[...] = value.astype(BF)
    normal, scale = row_stats(value)
    low = (normal * gain[...] + shift[...]).astype(BF)
    normed[...] = low
    grad_normed = None
    done = None
    coming = mm(low, w_up[:, :step], 1, 0)
    for start in range(0, hidden, step):
        cols = slice(start, start + step)
        pre = coming + b_up[:, cols]
        after = start + step
        if after < hidden:
            coming = mm(low, w_up[:, after : after + step], 1, 0)
        if done is not None:
            grad_normed = done if grad_normed is None else grad_normed + done
        out, slope = gelu_parts(pre)
        gelu_out[:, cols] = out.astype(BF)
        if after <= hidden // 2:
            grad_out = grad_gelu_low[:, cols]
        else:
            grad_out = grad_gelu_high[:, start - hidden // 2 : after - hidden // 2]
        back = (grad_out.astype(F32) * slope).astype(BF)
        grad_pre[:, cols] = back
        bias_sum[:, cols] += jnp.sum(back.astype(F32), axis=0, keepdims=True)
        done = mm(back, w_up[:, cols], 1, 1)
    grad_normed = grad_normed + done
    sums[0:1, :] += jnp.sum(grad_normed * normal, axis=0, keepdims=True)
    sums[1:2, :] += jnp.sum(grad_normed, axis=0, keepdims=True)
    length = info[2]
    live = usable_rows(rows, length)
    pooled = cot_pool[...] / length.astype(F32)
    final = (cot_act[0, 0].astype(F32) + pooled) * live
    total = final + norm_back(grad_normed, normal, scale, gain[...])
    total_low = total.astype(BF)
    grad_attn[...] = total_low
    grad_mixed[...] = mm(total_low, w_out[...], 1, 1).astype(BF)


def middle_rows(
    info, mixed, embedded, low, high, cot_act, cot_pool, w_out, gain, shift, w_up, b_up
):
    rows, width = mixed.shape
    hidden = w_up.shape[1]
    narrow = pl.BlockSpec((ROWS, width), lambda i, s: (i, 0))
    wide = pl.BlockSpec((ROWS, hidden), lambda i, s: (i, 0))
    part = pl.BlockSpec((ROWS, hidden // 2), lambda i, s: (i, 0))
    return call(
        middle_body,
        (rows // ROWS,),
        (info,),
        [
            narrow,
            narrow,
            part,
            part,
            pl.BlockSpec((1, 1, ROWS, width), lambda i, s: (0, 0, i, 0)),
            fixed((1, width)),
            fixed((width, width)),
            fixed((1, width)),
            fixed((1, width)),
            fixed((width, hidden)),
            fixed((1, hidden)),
        ],
        [narrow, narrow, wide, wide, narrow, narrow]
        + [
            pl.BlockSpec((8, width), lambda i, s: (0, 0)),
            pl.BlockSpec((1, hidden), lambda i, s: (0, 0)),
        ],
        [
            shape((rows, width), BF),
            shape((rows, width), BF),
            shape((rows, hidden), BF),
            shape((rows, hidden), BF),
            shape((rows, width), BF),
            shape((rows, width), BF),
            shape((8, width), F32),
            shape((1, hidden), F32),
        ],
        (mixed, embedded, low, high, cot_act, cot_pool, w_out, gain, shift, w_up, b_up),
        2 * rows * width * (2 * width + 2 * hidden),
    )


SAME_QUARTER = (3, 1, 2, 0)


def down_body(height, order, which, left, right_theirs, right_mine, theirs, mine):
    half = right_mine.shape[1]
    both = jnp.concatenate([right_theirs[...], right_mine[...]], axis=1)
    out = mm(left[...], both, 0, 0).astype(BF)
    folds, quarter = theirs.shape[1:3]
    for shard in range(quarter // height):
        for fold in range(folds):
            at = (shard * folds + fold) * height
            rows = slice(shard * height, (shard + 1) * height)
            theirs[0, fold, rows] = out[at : at + height, :half]
            mine[0, fold, rows] = out[at : at + height, half:]


def grad_down_halves(order, which, gelu_out, branch, first, count, height):
    rows, hidden = gelu_out.shape
    width = branch.shape[1]
    half = width // 2
    tall = hidden // 4
    block = (1, hidden // width, width // 4, half)
    return call(
        functools.partial(down_body, height),
        (count,),
        (order, which),
        [
            pl.BlockSpec((rows, tall), lambda j, o, w: (0, o[first + j])),
            pl.BlockSpec((rows, half), lambda j, o, w: (0, 1 - w[0])),
            pl.BlockSpec((rows, half), lambda j, o, w: (0, w[0])),
        ],
        [pl.BlockSpec(block, lambda j, o, w: (j, 0, 0, 0))] * 2,
        [shape((count,) + block[1:], BF)] * 2,
        (gelu_out, branch, branch),
        rows * hidden * half * count,
    )


def place_quarters(places, value, theirs, mine, rows=None):
    quarter = value.shape[0] // 4
    lanes = mine.shape[3]
    for i in range(4):
        block = value[i * quarter : (i + 1) * quarter].astype(BF)
        theirs[places[4 + i], 0, :quarter] = block[:, :lanes]
        mine[places[i], 0, :quarter] = block[:, lanes:]


def up_body(
    places, which, normed, pre_theirs, pre_mine, mixed, attn_theirs, attn_mine, theirs, mine
):
    step = pl.program_id(0)
    last = pl.num_programs(0) - 1

    @pl.when(step < last)
    def _():
        both = jnp.concatenate([pre_theirs[...], pre_mine[...]], axis=1)
        place_quarters(places, mm(normed[...], both, 0, 0), theirs, mine)

    @pl.when(step == last)
    def _():
        both = jnp.concatenate([attn_theirs[...], attn_mine[...]], axis=1)
        place_quarters(places, mm(mixed[...], both, 0, 0), theirs, mine)


def column_call(body, order, which, grid, lanes, quarter, specs, args, flops, vmem=40):
    return call(
        body,
        (grid,),
        (order, which),
        specs,
        [pl.BlockSpec((4, 1, quarter, lanes), lambda j, o, w: (0, j, 0, 0))] * 2,
        [shape((4, grid, quarter, lanes), BF)] * 2,
        args,
        flops,
        vmem=vmem,
    )


def grad_up_halves(order, which, normed, grad_pre, mixed, grad_attn):
    rows, width = normed.shape
    half = width // 2
    lanes = half
    steps = grad_pre.shape[1] // 2 // lanes

    def hidden_block(core):
        return pl.BlockSpec(
            (rows, lanes), lambda j, o, w: (0, core(w) * steps + jnp.minimum(j, steps - 1))
        )

    specs = [
        fixed((rows, width)),
        hidden_block(lambda w: 1 - w[0]),
        hidden_block(lambda w: w[0]),
        fixed((rows, width)),
        pl.BlockSpec((rows, half), lambda j, o, w: (0, 1 - w[0])),
        pl.BlockSpec((rows, half), lambda j, o, w: (0, w[0])),
    ]
    return column_call(
        up_body,
        order,
        which,
        steps + 1,
        lanes,
        width // 4,
        specs,
        (normed, grad_pre, grad_pre, mixed, grad_attn, grad_attn),
        4 * rows * width * (steps * lanes + half),
    )


def qkv_body(places, which, normed, grad_theirs, grad_mine, theirs, mine):
    both = jnp.concatenate([grad_theirs[...], grad_mine[...]], axis=1)
    place_quarters(places, mm(normed[...], both, 0, 0), theirs, mine)


def grad_qkv_halves(order, which, normed, grad_qkv):
    rows, width = normed.shape
    steps = 3
    lanes = grad_qkv.shape[1] // 2 // steps
    specs = [
        fixed((rows, width)),
        pl.BlockSpec((rows, lanes), lambda j, o, w: (0, (1 - w[0]) * steps + j)),
        pl.BlockSpec((rows, lanes), lambda j, o, w: (0, w[0] * steps + j)),
    ]
    return column_call(
        qkv_body,
        order,
        which,
        steps,
        lanes,
        width // 4,
        specs,
        (normed, grad_qkv, grad_qkv),
        4 * rows * width * steps * lanes,
    )


def kernel_body(
    places, which, pixels, grad_theirs, grad_mine, sums_one, sums_two, bias, theirs, mine
):
    both = jnp.concatenate([grad_theirs[...], grad_mine[...]], axis=1)
    out = mm(pixels[0, 0], both, 0, 0)
    place_quarters(places, out, theirs, mine)
    quarter = out.shape[0] // 4
    lanes = mine.shape[3]
    width = sums_one.shape[1] // 4
    folds = bias.shape[1] // 4 // width
    for i in range(4):
        cols = slice(i * width, (i + 1) * width)
        rows = [sums_one[0:1, cols], sums_one[1:2, cols], sums_two[0:1, cols], sums_two[1:2, cols]]
        for n in range(folds):
            at = (i * folds + n) * width
            rows.append(bias[:, at : at + width])
        rows.append(jnp.zeros((16 - len(rows), width), F32))
        block = jnp.concatenate(
            [jnp.concatenate(rows, axis=0), jnp.zeros((16, lanes - width), F32)], axis=1
        ).astype(BF)
        theirs[places[4 + i], 0, quarter:] = block
        mine[places[i], 0, quarter:] = block


def grad_kernel_halves(order, which, pixels, grad, sums_one, sums_two, bias):
    rows, patch = pixels.shape[2:]
    half = grad.shape[1] // 2
    specs = [
        pl.BlockSpec((1, 1, rows, patch), lambda j, o, w: (0, w[1], 0, 0)),
        pl.BlockSpec((rows, half), lambda j, o, w: (0, 1 - w[0])),
        pl.BlockSpec((rows, half), lambda j, o, w: (0, w[0])),
        fixed(sums_one.shape),
        fixed(sums_two.shape),
        fixed(bias.shape),
    ]
    return column_call(
        kernel_body,
        order,
        which,
        1,
        half,
        patch // 4 + 16,
        specs,
        (pixels, grad, grad, sums_one, sums_two, bias),
        4 * rows * patch * half,
        vmem=60,
    )


def first_back_body(grad_qkv, w_qkv, embedded, gain, grad_middle, out, sums):
    width = out.shape[1]
    pair = 2 * HD

    @pl.when(pl.program_id(0) == 0)
    def _():
        sums[...] = jnp.zeros_like(sums)

    grad = None
    for i in range(3):
        starts = range(i * pair, 3 * width, 3 * pair)
        value = jnp.concatenate([grad_qkv[:, at : at + pair] for at in starts], axis=1)
        part = mm(value, w_qkv[:, i * width : (i + 1) * width], 1, 1)
        grad = part if grad is None else grad + part
    normal, scale = row_stats(embedded[...].astype(F32))
    sums[0:1, :] += jnp.sum(grad * normal, axis=0, keepdims=True)
    sums[1:2, :] += jnp.sum(grad, axis=0, keepdims=True)
    out[...] = (grad_middle[...].astype(F32) + norm_back(grad, normal, scale, gain[...])).astype(BF)


def first_back(grad_qkv, w_qkv, embedded, gain, grad_middle):
    rows, width = embedded.shape
    narrow = pl.BlockSpec((ROWS, width), lambda i: (i, 0))
    return call(
        first_back_body,
        (rows // ROWS,),
        (),
        [
            pl.BlockSpec((ROWS, 3 * width), lambda i: (i, 0)),
            fixed(w_qkv.shape),
            narrow,
            fixed((1, width)),
            narrow,
        ],
        [narrow, pl.BlockSpec((8, width), lambda i: (0, 0))],
        [shape((rows, width), BF), shape((8, width), F32)],
        (grad_qkv, w_qkv, embedded, gain, grad_middle),
        2 * rows * width * 3 * width,
        vmem=58,
    )


def last_body(info, middle, gelu_out, w_down, activations, pooled):
    rows = middle.shape[0]
    length = info[2]

    @pl.when(pl.program_id(0) == 0)
    def _():
        pooled[...] = jnp.zeros_like(pooled)

    final = middle[...].astype(F32) + mm(gelu_out[...], w_down[...], 1, 0)
    final = final * usable_rows(rows, length)
    activations[0, 0] = final.astype(BF)
    pooled[0] += jnp.sum(final, axis=0, keepdims=True)

    @pl.when(pl.program_id(0) == pl.num_programs(0) - 1)
    def _():
        pooled[...] = pooled[...] / length.astype(F32)


def last_rows(info, middle, gelu_out, w_down):
    rows, width = middle.shape
    hidden = w_down.shape[0]
    return call(
        last_body,
        (rows // ROWS,),
        (info,),
        [
            pl.BlockSpec((ROWS, width), lambda i, s: (i, 0)),
            pl.BlockSpec((ROWS, hidden), lambda i, s: (i, 0)),
            fixed((hidden, width)),
        ],
        [
            pl.BlockSpec((1, 1, ROWS, width), lambda i, s: (0, 0, i, 0)),
            pl.BlockSpec((1, 1, width), lambda i, s: (0, 0, 0)),
        ],
        [shape((1, 1, rows, width), BF), shape((1, 1, width), F32)],
        (middle, gelu_out, w_down),
        2 * rows * width * hidden,
    )


def pixel_body(grad_embedded, kernel, pixel_grad):
    pixel_grad[0, 0] = mm(grad_embedded[...], kernel[...], 1, 1)


def pixel_rows(grad_embedded, kernel):
    rows, width = grad_embedded.shape
    patch = kernel.shape[0]
    return call(
        pixel_body,
        (rows // ROWS,),
        (),
        [pl.BlockSpec((ROWS, width), lambda i: (i, 0)), fixed((patch, width))],
        pl.BlockSpec((1, 1, ROWS, patch), lambda i: (0, 0, i, 0)),
        shape((1, 1, rows, patch), F32),
        (grad_embedded, kernel),
        2 * rows * width * patch,
    )


def base_body(order, order_far, which, resize, near, far, out, work):
    half = near.shape[2]
    quarter = near.shape[1]
    patch = resize.shape[1]
    for j in range(4):
        rows = pl.ds(pl.multiple_of(order[j] * quarter, quarter), quarter)
        work[which[0], rows, :] = near[j]
        rows = pl.ds(pl.multiple_of(order_far[j] * quarter, quarter), quarter)
        work[1 - which[0], rows, :] = far[j]
    for c in range(out.shape[0]):
        for h in range(2):
            out[c, :, h * half : (h + 1) * half] = mm(
                resize[...], work[h, c * patch : (c + 1) * patch, :], 1, 0
            )


def base_grad_of(order, order_far, which, resize, near, far, channels):
    pixels, patch = resize.shape
    _, quarter, half = near.shape
    return call(
        base_body,
        (1,),
        (order, order_far, which),
        [fixed(resize.shape), fixed(near.shape), fixed(far.shape)],
        fixed((channels, pixels, 2 * half)),
        shape((channels, pixels, 2 * half), F32),
        (resize, near, far),
        2 * channels * pixels * patch * 2 * half,
        scratch=[pltpu.VMEM((2, 4 * quarter, half), BF)],
    )


class Links:
    def __init__(self):
        self.parts = lax.axis_size("pix")
        self.count = lax.axis_size("tok")
        self.pix = lax.axis_index("pix")
        self.tok = lax.axis_index("tok")
        self.core = self.tok % 2
        self.chips = self.count // 2
        self.near = 1 + self.core
        self.far = 2 - self.core

    def swap(self, value, partner):
        pairs = []
        for p in range(self.parts):
            for t in range(self.count):
                q, u = partner(p, t)
                pairs.append((p * self.count + t, q * self.count + u))
        return lax.ppermute(value, ("pix", "tok"), pairs)

    def core_swap(self, value):
        return self.swap(value, lambda p, t: (p, t ^ 1))

    def first_swap(self, value):
        return self.swap(value, lambda p, t: (p ^ (1 + t % 2), t))

    def second_swap(self, value):
        return self.swap(value, lambda p, t: (p ^ (2 - t % 2), t))

    def chip_swap(self, value, bit):
        bits = self.chips.bit_length() - 1

        def partner(p, t):
            return p, t ^ (2 << (bit if t % 2 == 0 else bits - 1 - bit))

        return self.swap(value, partner)

    def quarters(self, near, far):
        pix = self.pix
        return jnp.stack([pix ^ near, pix ^ 3, pix, pix ^ far]).astype(jnp.int32)


def places_of(order):
    return jnp.argmax(order[None, :] == jnp.arange(4)[:, None], axis=1).astype(jnp.int32)


def together(*values):
    return lax.optimization_barrier(values)


def add(a, b, dtype=BF):
    return (a.astype(F32) + b.astype(F32)).astype(dtype)


def combine(arrived, mine):
    return add(arrived[:2], mine[:2]), add(arrived[2:], mine[2:])


class Order:
    def __init__(self):
        self.last = ()

    def __call__(self, work, *values, keep=False):
        flat, tree = jax.tree.flatten(values)
        count = len(flat)
        if self.last:
            flat = list(together(*flat, *self.last))[:count]
        result = work(*jax.tree.unflatten(tree, flat))
        if not keep:
            self.last = tuple(jax.tree.leaves(result))
        return result


class Chain:
    def __init__(self, order, links, away, keep):
        self.order, self.links = order, links
        self.stage = 0
        self.bits = links.chips.bit_length() - 1
        self.arrived = links.first_swap(away)
        self.staying = keep

    def advance(self):
        links, stage, bits = self.links, self.stage, self.bits
        if stage > bits + 1:
            return

        def quarters(arrived, staying):
            return add(arrived[1], staying[1]), add(arrived[0], staying[0])

        def split(value, bit):
            top = links.core == 1
            left = value.shape[0] // 2
            place = jnp.where(top, bits - 1 - bit, bit)
            own = (links.tok >> (place + 1)) & 1
            low = value.reshape(left, 2, *value.shape[1:])
            high = value.reshape(2, left, *value.shape[1:])

            def pick(which):
                return jnp.where(
                    top,
                    lax.dynamic_index_in_dim(high, which, 0, keepdims=False),
                    lax.dynamic_index_in_dim(low, which, 1, keepdims=False),
                )

            return pick(1 - own), pick(own)

        def halves(value):
            chip = links.tok // 2

            def pick(*masks):
                return jnp.stack(
                    [
                        lax.dynamic_index_in_dim(value, chip ^ mask, 0, keepdims=False)
                        for mask in masks
                    ]
                )

            return pick(links.near, 3), pick(0, links.far)

        def pix_sum(arrived, staying):
            value = add(arrived, staying)
            blocks, rows, lanes = value.shape
            value = value.reshape(blocks, links.chips, rows // links.chips, lanes)
            value = value.transpose(1, 0, 2, 3)
            return halves(value) if bits == 2 else split(value, 0)

        def chip_sum(arrived, staying):
            if bits == 2:
                return quarters(arrived, staying)
            return split(add(arrived, staying), stage - 1)

        def last_sum(arrived, staying):
            value = add(arrived, staying, F32)
            return value if bits == 2 else value[0]

        if stage > bits:
            self.value = self.order(last_sum, self.arrived, self.staying, keep=True)
        else:
            work = quarters if stage == 0 else pix_sum if stage == 1 else chip_sum
            leaving, self.staying = self.order(work, self.arrived, self.staying)
            if stage == 0:
                self.arrived = links.second_swap(leaving)
            else:
                self.arrived = links.chip_swap(leaving, stage - 1)
        self.stage += 1

    def finish(self):
        while self.stage <= self.bits + 1:
            self.advance()
        return self.value


def own_rows(links, value):
    blocks, rows, lanes = value.shape
    pair = value.reshape(blocks, 2, rows // 2, lanes)
    mine = lax.dynamic_index_in_dim(pair, links.core, 1, keepdims=False)
    arrived = links.core_swap(
        lax.dynamic_index_in_dim(pair, 1 - links.core, 1, keepdims=False)
    )
    first = links.core == 0
    return jnp.where(first, mine, arrived), jnp.where(first, arrived, mine)


def local(
    pixels,
    lengths,
    base_kernel,
    resize,
    gain_one,
    shift_one,
    w_qkv,
    w_out,
    gain_two,
    shift_two,
    w_up,
    b_up,
    w_down,
    cot_act,
    cot_pool,
):
    links = Links()
    turn = Order()
    seq_len = pixels.shape[2]
    width = w_qkv.shape[0]
    hidden = w_up.shape[1]
    channels = base_kernel.shape[0]
    half = width // 2
    core = links.core
    own_length = lax.dynamic_index_in_dim(lengths[0], links.pix, 0, keepdims=False)
    info = jnp.stack([links.pix, core, own_length]).astype(jnp.int32)
    mine = jnp.stack([core, links.pix]).astype(jnp.int32)
    order = links.quarters(links.near, links.far)
    order_theirs = links.quarters(links.far, links.near)
    places = jnp.concatenate([places_of(order), places_of(order_theirs)])
    gain_one, shift_one = gain_one[None], shift_one[None]
    gain_two, shift_two, b_up = gain_two[None], shift_two[None], b_up[None]
    cot_pool = cot_pool[0]

    piece = partial_kernel(resize, base_kernel)
    piece = add(links.first_swap(piece), piece)
    branch, gelu_low = cot_branch(info, cot_act, cot_pool, w_down, 0)
    piece, branch, gelu_low = together(piece, branch, gelu_low)
    piece = add(links.second_swap(piece), piece)
    (gelu_high,) = cot_branch(info, cot_act, cot_pool, w_down, 1)
    piece, gelu_high = together(piece, gelu_high)
    other = links.core_swap(piece)
    kernel = jnp.concatenate(
        [jnp.where(core == 0, piece, other), jnp.where(core == 0, other, piece)], axis=1
    )

    lane = jnp.arange(2 * HD)[None, None, :]
    slot = jnp.array([HD, 0])[:, None, None]
    blocked = (jnp.arange(seq_len) >= own_length)[None, :, None] & (lane == slot)
    extra = jnp.where(blocked, -1e30, 0.0).astype(BF)

    embedded, normed, qkv = embed_rows(info, pixels, kernel, gain_one, shift_one, w_qkv)
    probs, mixed, inverse = attend(qkv, extra)
    (
        middle,
        normed_two,
        gelu_out,
        grad_pre,
        grad_attn,
        grad_mixed,
        sums_two,
        bias_sum,
    ) = middle_rows(
        info,
        mixed,
        embedded,
        gelu_low,
        gelu_high,
        cot_act,
        cot_pool,
        w_out,
        gain_two,
        shift_two,
        w_up,
        b_up,
    )

    shard = width // (links.parts * links.chips)
    up_theirs, up_mine = turn(
        lambda *a: grad_up_halves(places, mine, *a), normed_two, grad_pre, mixed, grad_attn
    )
    up_arrived = links.core_swap(up_theirs)
    away_theirs, away_mine = turn(
        lambda *a: grad_down_halves(order, mine, *a, 0, 2, shard), gelu_out, branch
    )
    away_arrived = links.core_swap(away_theirs)
    up_arrived, gelu_last = together(up_arrived, gelu_out)
    keep_theirs, keep_mine = turn(
        lambda *a: grad_down_halves(order, mine, *a, 2, 2, shard), gelu_last, branch
    )
    keep_arrived = links.core_swap(keep_theirs)
    def combine_wide(up_arrived, up_mine, away_arrived, away_mine, keep_arrived, keep_mine):
        up_away, up_keep = combine(up_arrived, up_mine)
        away = add(jnp.stack([keep_arrived[1], away_arrived[1]]), away_mine)
        keep = add(jnp.stack([keep_arrived[0], away_arrived[0]]), keep_mine)
        return (
            jnp.concatenate([up_away, away], axis=1),
            jnp.concatenate([up_keep, keep], axis=1),
        )

    wide = Chain(
        turn,
        links,
        *turn(
            combine_wide, up_arrived, up_mine, away_arrived, away_mine, keep_arrived, keep_mine
        ),
    )

    every = width // (2 * HD)
    cuts = [every // 3 * n for n in range(3)] + [every]

    def back(n, before):
        return turn(
            lambda probs, *a: attend_back(
                probs, qkv, grad_mixed, mixed, inverse, cuts[n], cuts[n + 1] - cuts[n], *a
            ),
            probs,
            before,
        )

    grad_qkv = back(0, None)
    grad_qkv = back(1, grad_qkv)
    grad_qkv = back(2, grad_qkv)
    wide.advance()

    three_theirs, three_mine = turn(
        lambda *a: grad_qkv_halves(places, mine, *a), normed, grad_qkv
    )
    three_arrived = links.core_swap(three_theirs)

    grad_embedded, sums_one = turn(
        lambda *a: first_back(*a, w_qkv, embedded, gain_one, grad_attn), grad_qkv
    )
    three_away, three_keep = turn(combine, three_arrived, three_mine)
    three = Chain(turn, links, three_away, three_keep)
    kernel_theirs, kernel_mine = turn(
        lambda *a: grad_kernel_halves(places, mine, pixels, *a, sums_two, bias_sum),
        grad_embedded,
        sums_one,
    )
    arrived = links.core_swap(kernel_theirs)
    wide.advance()
    away, keep = turn(combine, arrived, kernel_mine)
    arrived = links.first_swap(away)
    leaving, staying = turn(
        lambda a, b: (add(a[1], b[1]), add(a[0], b[0])), arrived, keep
    )
    arrived = links.second_swap(leaving)
    three.advance()
    quarter = turn(add, arrived, staying)
    arrived = links.chip_swap(quarter, 0)
    pixel_grad = turn(pixel_rows, grad_embedded, kernel)
    wide.advance()
    quarter = turn(add, arrived, quarter)
    arrived = links.chip_swap(quarter, 1)
    three.advance()
    activations, pooled = turn(
        lambda *a: last_rows(info, *a), middle, gelu_out, w_down
    )
    quarter = turn(add, arrived, quarter)
    for bit in range(2, links.chips.bit_length() - 1):
        arrived = links.chip_swap(quarter, bit)
        quarter = turn(add, arrived, quarter)
    vectors = quarter[0, -16:, : width // links.parts].astype(F32)
    quarter = quarter[0, :-16]
    arrived = links.second_swap(quarter)
    wide.advance()
    three.advance()
    pair = turn(lambda a, b: jnp.stack([a, b]), quarter, arrived)
    arrived = links.first_swap(pair)
    full = turn(lambda a, b: jnp.concatenate([a, b], axis=0), arrived, pair)
    arrived = links.core_swap(full)
    base_grad = turn(
        lambda *a: base_grad_of(order, order_theirs, mine, resize, *a, channels), full, arrived
    )
    wide, three = wide.finish(), three.finish()

    height = width // (links.parts * links.count)
    tall = hidden // (links.parts * links.count)
    folds = hidden // width
    wide_low, wide_high = own_rows(links, wide[: folds + 1])
    grad_up = jnp.concatenate([*wide_low[:folds], *wide_high[:folds]], axis=1)
    grad_out = jnp.concatenate([wide_low[folds], wide_high[folds]], axis=1)
    part = wide[folds + 1 :].reshape(2, -1, half)
    down_mine = lax.dynamic_index_in_dim(part, core, 0, keepdims=False)
    down_arrived = links.core_swap(
        lax.dynamic_index_in_dim(part, 1 - core, 0, keepdims=False)
    )
    down = jnp.concatenate(
        [
            jnp.where(core == 0, down_mine, down_arrived),
            jnp.where(core == 0, down_arrived, down_mine),
        ],
        axis=1,
    )
    three_low, three_high = own_rows(links, three)
    three_low = jnp.concatenate(list(three_low), axis=1)
    three_high = jnp.concatenate(list(three_high), axis=1)
    pair = 2 * HD
    pieces = []
    for i in range(3):
        for value in (three_low, three_high):
            for at in range(i * pair, value.shape[1], 3 * pair):
                pieces.append(value[:, at : at + pair])
    grad_qkv = jnp.concatenate(pieces, axis=1)
    small = lax.dynamic_slice_in_dim(vectors[:4], links.tok * height, height, 1)
    grad_bias = lax.dynamic_slice_in_dim(
        vectors[4 : 4 + folds].reshape(-1), links.tok * tall, tall, 0
    )
    return (
        activations,
        pooled,
        pixel_grad,
        base_grad,
        small[0],
        small[1],
        grad_qkv,
        grad_out,
        small[2],
        small[3],
        grad_up,
        grad_bias,
        down,
    )


def solution(mesh):
    placed = (
        P("tok", None, None, None),
        P("tok", None),
        P(None, "pix", None),
        P("pix", None),
        P(),
        P(),
        P(),
        P(),
        P(),
        P(),
        P(),
        P(),
        P(),
        P("tok", "pix", None, None),
        P("tok", "pix", None),
    )
    return jax.shard_map(
        local,
        mesh=mesh,
        in_specs=placed,
        out_specs=(
            P("tok", "pix", None, None),
            P("tok", "pix", None),
            P("tok", "pix", None, None),
            P(None, "pix", None),
            P(("pix", "tok")),
            P(("pix", "tok")),
            P(("pix", "tok"), None),
            P(("pix", "tok"), None),
            P(("pix", "tok")),
            P(("pix", "tok")),
            P(("pix", "tok"), None),
            P(("pix", "tok")),
            P(("pix", "tok"), None),
        ),
        check_vma=False,
    )
```
